32 devices in a mesh: atom: 4 (over x, core), tm: 8 (over z, y).
Axes of the slice: x: 2, y: 2, z: 4, core: 2. Of those that a mesh axis runs over, the one named last changes fastest.
Arguments:
- positions: int32 [64, 3, 8192], P('tm', None, 'atom'), may hold values from 0 to 131071, as said below
- velocity: bfloat16 [64, 3, 8192], P('tm', None, 'atom'), may hold values from -5 to 5
Outputs:
- correlation: float32 [4, 16, 32768], P(None, None, ('atom', 'tm'))
The draws below stay inside these ranges and needn't reach their ends.
Inputs may be any that keep to these rules, and one draw needn't show every extreme that they name: `positions`: along each axis an atom's coordinate changes between consecutive frames by at most 1536 lattice points, counted modulo 131072.
All inputs are finite; a program needn't handle non-finite values.
Results may differ from the reference program's by a relative error of at most 0.00075.
Values may be sent and summed in bfloat16 or wider, within the bound.
A program may use at most 128 MiB of HBM per device.

```python
import math
import jax
import jax.numpy as jnp
from jax import lax

KX = 32
KY = 32
KZ = 32
LAGS = 16
LATTICE = 131072
STEP = 1536
ATOMS = 8192
FRAMES = 64


def walk_steps(key):
    walk_key = jax.random.fold_in(key, 11)
    first_key, step_key, speed_key = jax.random.split(walk_key, 3)
    anchor = jax.random.randint(first_key, (1, 3, ATOMS), 0, LATTICE, dtype=jnp.int32)
    displacement = jax.random.randint(step_key, (FRAMES, 3, ATOMS), -STEP, STEP + 1, dtype=jnp.int32)
    return (anchor, displacement, speed_key)


def draw_positions(key, part):
    anchor, displacement, speed_key = walk_steps(key)
    travelled = jnp.cumsum(displacement, 0) - displacement
    return (anchor + travelled) % LATTICE


def draw_velocity(key, part):
    anchor, displacement, speed_key = walk_steps(key)
    drift_key = jax.random.fold_in(speed_key, 0)
    drift_speed = 0.5 * jnp.clip(jax.random.normal(drift_key, (1, 3, ATOMS), jnp.float32), -4.0, 4.0)
    moving = drift_speed + 0.5 * displacement.astype(jnp.float32) / STEP
    return moving.astype(jnp.bfloat16)


def setup_inputs(seed: int = 0) -> dict:
    splits = jax.random.split(jax.random.key(seed), 3)
    return {
        "positions": draw_positions(jax.random.fold_in(splits[2], 71), 0),
        "velocity": draw_velocity(jax.random.fold_in(splits[2], 71), 0),
    }


def wave_numbers(number, offset, extent):
    counter = jnp.arange(number, dtype=jnp.int32) + offset
    return counter - extent // 2 + (counter >= extent // 2).astype(jnp.int32)


def phase_pair(coords, numbers):
    folded = (numbers[None, :, None] * coords[:, None, :]) % LATTICE
    angles = folded.astype(jnp.float32) * (2.0 * math.pi / LATTICE)
    return jnp.cos(angles), jnp.sin(angles)


def operands(positions, velocity, kx_first, kx_number):
    frame_count, atom_count = positions.shape[0], positions.shape[2]
    cos_x, sin_x = phase_pair(positions[:, 0], wave_numbers(kx_number, kx_first, KX))
    cos_y, sin_y = phase_pair(positions[:, 1], wave_numbers(KY, 0, KY))
    cos_z, sin_z = phase_pair(positions[:, 2], wave_numbers(KZ, 0, KZ))
    real_xy = cos_x[:, :, None] * cos_y[:, None] - sin_x[:, :, None] * sin_y[:, None]
    imag_xy = cos_x[:, :, None] * sin_y[:, None] + sin_x[:, :, None] * cos_y[:, None]
    left_side = jnp.concatenate([real_xy, imag_xy], 1)
    left_side = left_side.reshape(frame_count, 2 * kx_number * KY, atom_count).astype(jnp.bfloat16)
    weights = jnp.concatenate([jnp.ones((frame_count, 1, atom_count), jnp.float32), velocity.astype(jnp.float32)], 1)
    right_side = jnp.stack([cos_z[:, None] * weights[:, :, None], sin_z[:, None] * weights[:, :, None]], 2)
    right_side = right_side.reshape(frame_count, -1, atom_count).astype(jnp.bfloat16)
    return left_side, right_side


def finish(raw, row_count):
    frame_count = raw.shape[0]
    split = raw.reshape(frame_count, 2, row_count, -1, 2, KZ)
    real_part = split[:, 0, :, :, 0] - split[:, 1, :, :, 1]
    imag_part = split[:, 0, :, :, 1] + split[:, 1, :, :, 0]
    joined = jnp.stack([real_part, imag_part], 3)
    return jnp.transpose(joined, (1, 0, 2, 3, 4)).reshape(row_count, -1)


def mode_rows(positions, velocity, kx_first, kx_number, block_limit):
    frame_count, atom_count = positions.shape[0], positions.shape[2]
    atom_block = math.gcd(atom_count, block_limit)
    row_count = kx_number * KY
    channels = (velocity.shape[1] + 1) * 2 * KZ

    def accumulate(running, block_index):
        pos_block = lax.dynamic_slice_in_dim(positions, block_index * atom_block, atom_block, 2)
        vel_block = lax.dynamic_slice_in_dim(velocity, block_index * atom_block, atom_block, 2)
        left_side, right_side = operands(pos_block, vel_block, kx_first, kx_number)
        product = jnp.einsum("fra,fca->frc", left_side.astype(jnp.float32), right_side.astype(jnp.float32))
        return running + product, None

    initial = jnp.zeros((frame_count, 2 * row_count, channels), jnp.float32)
    running = lax.scan(accumulate, initial, jnp.arange(atom_count // atom_block, dtype=jnp.int32))[0]
    return finish(running, row_count)


def reference(positions, velocity):
    frame_count, atom_count = positions.shape[0], positions.shape[2]

    def one_frame(frame_pair):
        return mode_rows(frame_pair[0][None], frame_pair[1][None], 0, KX, 2048)

    modes = lax.map(one_frame, (positions, velocity))
    modes = modes.reshape(frame_count, KX * KY, -1, 2, KZ)
    results = []
    for lag_index in range(LAGS):
        product = modes[: frame_count - lag_index] * modes[lag_index:]
        results.append(jnp.sum(product, axis=(0, 3)) / (atom_count * (frame_count - lag_index)))
    stacked = jnp.stack(results)
    return jnp.transpose(stacked, (2, 0, 1, 3)).reshape(stacked.shape[2], LAGS, -1)
```

```python
import functools
import math

import jax
import jax.numpy as jnp
from jax import lax
from jax.experimental import pallas as pl
from jax.experimental.pallas import tpu as pltpu
from jax.sharding import PartitionSpec as P

KX = 32
KY = 32
KZ = 32
LAGS = 16
LATTICE = 131072
QUARTER = LATTICE // 4
HALF_Z = KZ // 2
COMPS = 4
LANES = 128
VMEM = 56 * 1024 * 1024


def wave(q, extent):
    return q - extent // 2 + (1 if q >= extent // 2 else 0)


def sincos(n):
    n = jnp.bitwise_and(n, LATTICE - 1)
    quadrant = jnp.right_shift(n + QUARTER // 2, 15)
    x = (n - jnp.left_shift(quadrant, 15)).astype(jnp.float32) * (2.0 * math.pi / LATTICE)
    y = x * x
    s = y * (1.0 / 362880.0) - 1.0 / 5040.0
    s = s * y + 1.0 / 120.0
    s = s * y - 1.0 / 6.0
    s = s * y * x + x
    c = y * (1.0 / 40320.0) - 1.0 / 720.0
    c = c * y + 1.0 / 24.0
    c = c * y - 0.5
    c = c * y + 1.0
    odd = jnp.bitwise_and(quadrant, 1) == 1
    cos = jnp.where(odd, s, c)
    sin = jnp.where(odd, c, s)
    cos = jnp.where(jnp.bitwise_and(quadrant + 1, 2) == 2, -cos, cos)
    sin = jnp.where(jnp.bitwise_and(quadrant, 2) == 2, -sin, sin)
    return cos, sin


def times(a, b):
    return a[0] * b[0] - a[1] * b[1], a[0] * b[1] + a[1] * b[0]


def plus_minus(a, b):
    cc, ss, cs, sc = a[0] * b[0], a[1] * b[1], a[0] * b[1], a[1] * b[0]
    return (cc - ss, sc + cs), (cc + ss, sc - cs)


def powers(e1):
    e = {1: e1}
    e[2] = times(e1, e1)
    e[3] = times(e[2], e1)
    e[4] = times(e[2], e[2])
    e[8] = times(e[4], e[4])
    e[12], _ = plus_minus(e[8], e[4])
    for d in (1, 2, 3):
        e[8 + d], e[8 - d] = plus_minus(e[8], e[d])
    e[16] = times(e[8], e[8])
    for d in (1, 2, 3):
        _, e[16 - d] = plus_minus(e[16], e[d])
    return e


def prepare(pos, xs, yc, ys, zc, zs, lanes, frames, block, first_w, group, y_waves):
    middle = (group - 1) // 2

    def step(i, _):
        at = pl.ds(pl.multiple_of(i * block, block), block)
        n = pos(0, at)
        base = sincos((first_w + middle) * n)
        xs[0, :, at], xs[1, :, at] = base
        e1 = sincos(n)
        e = {1: e1}
        for d in range(2, group - middle):
            e[d] = times(e[d - 1], e1)
        for d in range(1, group - middle):
            xs[2 * d, :, at], xs[2 * d + 1, :, at] = e[d]
        e = powers(sincos(pos(1, at)))
        for row, w in enumerate(y_waves):
            c, s = e[abs(w)]
            yc[i, row * frames : (row + 1) * frames, :] = c
            ys[i, row * frames : (row + 1) * frames, :] = s if w > 0 else -s
        e = powers(sincos(pos(2, at)))
        for w in range(1, HALF_Z + 1):
            c, s = e[w]
            zc[i, (w - 1) * frames : w * frames, :] = c
            zs[i, (w - 1) * frames : w * frames, :] = s
        return 0

    lax.fori_loop(0, lanes // block, step, 0)


def frame_product(f, vel, xs, yc, ys, zc, zs, lanes, frames, block, group, rows):
    middle = (group - 1) // 2
    total = None
    steps = block // LANES

    def pick(ref, i):
        parts = [ref[i * steps + k, pl.ds(f, rows, stride=frames), :] for k in range(steps)]
        return jnp.concatenate(parts, 1)

    for i in range(lanes // block):
        at = pl.ds(i * block, block)
        y = (pick(yc, i), pick(ys, i))
        x = [xs[j, pl.ds(f, 1), at] for j in range(2 * (group - middle))]
        mid = times((x[0], x[1]), y)
        e = {middle: mid}
        for d in range(1, group - middle):
            up, down = plus_minus(mid, (x[2 * d], x[2 * d + 1]))
            e[middle + d] = up
            if middle - d >= 0:
                e[middle - d] = down
        left = []
        for j in range(group):
            left += [e[j][0].astype(jnp.bfloat16), e[j][1].astype(jnp.bfloat16)]
        left = jnp.concatenate(left, 0)
        right = []
        for z_ref in (zc, zs):
            z = pick(z_ref, i)
            right.append(z.astype(jnp.bfloat16))
            for a in range(COMPS - 1):
                right.append((z * vel(a, f, at)).astype(jnp.bfloat16))
        right = jnp.concatenate(right, 0)
        part = lax.dot_general(
            left, right, (((1,), (1,)), ((), ())), preferred_element_type=jnp.float32
        )
        total = part if total is None else total + part
    return total


def combine(raw, group, rows):
    lane = lax.broadcasted_iota(jnp.int32, (rows, LANES), 1)
    sign = jnp.where(lane < LANES // 2, -1.0, 1.0)
    out = []
    for j in range(group):
        re = raw[2 * j * rows : (2 * j + 1) * rows]
        im = raw[(2 * j + 1) * rows : (2 * j + 2) * rows]
        turned = pltpu.roll(im, LANES // 2, 1) * sign
        out.append(jnp.concatenate([re + turned, re - turned], 1))
    return out


def modes_kernel(dims, pos_ref, vel_ref, out_ref, xs, yc, ys, zc, zs, total):
    frames, chunk, group, rows, y_waves = dims
    first = lax.axis_index("atom") * group
    first_w = first - KX // 2 + (first >= KX // 2).astype(jnp.int32)
    total[...] = jnp.zeros_like(total)

    def chunk_step(c, _):
        base = pl.multiple_of(c * chunk, chunk)
        prepare(
            lambda a, at: pos_ref[a, :, pl.ds(pl.multiple_of(base + at.start, LANES), at.size)],
            xs, yc, ys, zc, zs, chunk, frames, LANES, first_w, group, y_waves,
        )

        def frame_step(f, _):
            total[f] += frame_product(
                f,
                lambda a, f, at: vel_ref[a, pl.ds(f, 1), pl.ds(pl.multiple_of(base + at.start, LANES), at.size)],
                xs, yc, ys, zc, zs, chunk, frames, 4 * LANES, group, rows,
            )
            return 0

        lax.fori_loop(0, frames, frame_step, 0)
        return 0

    lax.fori_loop(0, pos_ref.shape[2] // chunk, chunk_step, 0)

    def emit(f, _):
        for j, block in enumerate(combine(total[f], group, rows)):
            out_ref[j, f] = block.astype(out_ref.dtype)
        return 0

    lax.fori_loop(0, frames, emit, 0)


def modes_call(pos, vel, group, rows, y_waves):
    frames, atoms = pos.shape[1], pos.shape[2]
    chunk = math.gcd(atoms, 2048)
    kernel = functools.partial(modes_kernel, (frames, chunk, group, rows, y_waves))
    whole = pl.BlockSpec(memory_space=pltpu.VMEM)
    return pl.pallas_call(
        kernel,
        out_shape=jax.ShapeDtypeStruct((group, frames, rows, 2 * LANES), jnp.bfloat16),
        in_specs=[whole, whole],
        out_specs=whole,
        scratch_shapes=[
            pltpu.VMEM((2 * (group - (group - 1) // 2), frames, chunk), jnp.float32),
            pltpu.VMEM((chunk // LANES, rows * frames, LANES), jnp.float32),
            pltpu.VMEM((chunk // LANES, rows * frames, LANES), jnp.float32),
            pltpu.VMEM((chunk // LANES, HALF_Z * frames, LANES), jnp.float32),
            pltpu.VMEM((chunk // LANES, HALF_Z * frames, LANES), jnp.float32),
            pltpu.VMEM((frames, group * 2 * rows, LANES), jnp.float32),
        ],
        compiler_params=pltpu.CompilerParams(vmem_limit_bytes=VMEM),
        name="modes",
    )(pos, vel)


def fold_matrices():
    lane = lax.broadcasted_iota(jnp.int32, (LANES, LANES), 0)
    goal = lax.broadcasted_iota(jnp.int32, (LANES, LANES), 1)
    comp = jnp.right_shift(jnp.bitwise_and(lane, 63), 4)
    step = jnp.bitwise_and(lane, HALF_Z - 1)
    own = []
    for qz in (KZ // 2 + step, KZ // 2 - 1 - step):
        own.append(comp * KZ + qz)
    mirror = [comp * KZ + KZ - 1 - (t - comp * KZ) for t in own]
    return [[(goal == t).astype(jnp.float32).astype(jnp.bfloat16) for t in side] for side in (own, mirror)]


def exact_dot(x, matrix):
    high = x.astype(jnp.bfloat16)
    low = (x - high.astype(jnp.float32)).astype(jnp.bfloat16)
    return jnp.dot(high, matrix, preferred_element_type=jnp.float32) + jnp.dot(
        low, matrix, preferred_element_type=jnp.float32
    )


def correlate(series, wide, sums, frames, rows, atoms):
    tall = min(8, rows)
    slots = 2 * (rows // tall)

    def widen(t, _):
        block = series(t).astype(jnp.float32)
        for slot in range(slots):
            r, half = divmod(slot, 2)
            wide[slot, t] = block[r * tall : (r + 1) * tall, half * LANES : (half + 1) * LANES]
        return 0

    lax.fori_loop(0, frames, widen, 0)
    for slot in range(slots):
        r, half = divmod(slot, 2)
        window = [wide[slot, t] for t in range(LAGS)]
        acc = [None] * LAGS
        for t in range(frames):
            for lag in range(min(LAGS, frames - t)):
                product = window[0] * window[lag]
                acc[lag] = product if acc[lag] is None else acc[lag] + product
            window = window[1:]
            if t + LAGS < frames:
                window.append(wide[slot, t + LAGS])
        for lag in range(LAGS):
            sums[half, lag * rows + r * tall : lag * rows + (r + 1) * tall, :] = acc[lag] * (
                1.0 / (atoms * (frames - lag))
            )


def arrange(sums, folded, own_ref, mirror_ref, rows):
    own_fold, mirror_fold = fold_matrices()
    groups = max(1, rows // 4)
    per = rows // groups
    lane = lax.broadcasted_iota(jnp.int32, (LAGS, LANES), 1)
    block = jnp.right_shift(lane, 5)
    for fold, out_ref, flip in ((own_fold, own_ref, False), (mirror_fold, mirror_ref, True)):
        folded[...] = exact_dot(sums[0], fold[0]) + exact_dot(sums[1], fold[1])
        for g in range(groups):
            parts = [folded[pl.ds(g * per + i, LAGS, stride=rows), :] for i in range(per)]
            if flip:
                parts = parts[::-1]
            goal = groups - 1 - g if flip else g
            for c in range(COMPS):
                out = jnp.zeros((LAGS, LANES), jnp.float32)
                for i in range(per):
                    shift = ((i - c) * KZ) % LANES
                    part = parts[i] if shift == 0 else pltpu.roll(parts[i], shift, 1)
                    out = jnp.where(block == i, part, out)
                out_ref[c, :, goal * LANES : goal * LANES + LANES] = out


def correlate_kernel(dims, series_ref, own_ref, mirror_ref, wide, sums, folded):
    frames, rows, atoms = dims
    correlate(lambda t: series_ref[t], wide, sums, frames, rows, atoms)
    arrange(sums, folded, own_ref, mirror_ref, rows)


def correlate_call(series, atoms):
    frames, rows = series.shape[0], series.shape[1]
    tall = min(8, rows)
    whole = pl.BlockSpec(memory_space=pltpu.VMEM)
    out = jax.ShapeDtypeStruct((COMPS, LAGS, rows * KZ), jnp.float32)
    return pl.pallas_call(
        functools.partial(correlate_kernel, (frames, rows, atoms)),
        out_shape=(out, out),
        in_specs=[whole],
        out_specs=(whole, whole),
        scratch_shapes=[
            pltpu.VMEM((2 * (rows // tall), frames, tall, LANES), jnp.float32),
            pltpu.VMEM((2, LAGS * rows, LANES), jnp.float32),
            pltpu.VMEM((LAGS * rows, LANES), jnp.float32),
        ],
        compiler_params=pltpu.CompilerParams(vmem_limit_bytes=VMEM),
        name="correlate",
    )(series)


def per_device(positions, velocity):
    atom_ways = lax.axis_size("atom")
    time_ways = lax.axis_size("tm")
    ways = atom_ways * time_ways
    frames = positions.shape[0]
    atoms = positions.shape[2] * atom_ways
    owned = KX * KY // ways
    rows = owned // 2
    group = KX // atom_ways
    y_waves = [wave(q, KY) for q in range(KY) if q % owned >= rows]
    pos = lax.all_gather(positions, "atom", axis=2, tiled=True)
    vel = lax.all_gather(velocity, "atom", axis=2, tiled=True)
    pos = jnp.transpose(pos, (1, 0, 2))
    vel = jnp.transpose(vel, (1, 0, 2)).astype(jnp.float32)
    modes = modes_call(pos, vel, group, KY // 2, y_waves)
    split = KY // owned
    modes = modes.reshape(group, frames, split, rows, 2 * LANES)
    modes = jnp.transpose(modes, (0, 2, 1, 3, 4)).reshape(time_ways, frames, rows, 2 * LANES)
    series = lax.all_to_all(modes, "tm", split_axis=0, concat_axis=0, tiled=True)
    own, mirror = correlate_call(series.reshape(time_ways * frames, rows, 2 * LANES), atoms)
    mirror = lax.ppermute(mirror, ("atom", "tm"), [(b, ways - 1 - b) for b in range(ways)])
    return jnp.concatenate([mirror, own], 2)


def solution(mesh):
    in_specs = (P("tm", None, "atom"), P("tm", None, "atom"))
    out_specs = P(None, None, ("atom", "tm"))
    return jax.shard_map(
        per_device, mesh=mesh, in_specs=in_specs, out_specs=out_specs, check_vma=False
    )
```

```python
import functools
import math

import jax
import jax.numpy as jnp
from jax import lax
from jax.experimental import pallas as pl
from jax.experimental.pallas import tpu as pltpu
from jax.sharding import PartitionSpec as P

KX = 32
KY = 32
KZ = 32
LAGS = 16
LATTICE = 131072
QUARTER = LATTICE // 4
HALF_Z = KZ // 2
COMPS = 4
LANES = 128
VMEM = 56 * 1024 * 1024
WIRE = jnp.bfloat16


def wave(q, extent):
    return q - extent // 2 + (1 if q >= extent // 2 else 0)


def sincos(n):
    n = jnp.bitwise_and(n, LATTICE - 1)
    quadrant = jnp.right_shift(n + QUARTER // 2, 15)
    x = (n - jnp.left_shift(quadrant, 15)).astype(jnp.float32) * (2.0 * math.pi / LATTICE)
    y = x * x
    s = y * (1.0 / 362880.0) - 1.0 / 5040.0
    s = s * y + 1.0 / 120.0
    s = s * y - 1.0 / 6.0
    s = s * y * x + x
    c = y * (1.0 / 40320.0) - 1.0 / 720.0
    c = c * y + 1.0 / 24.0
    c = c * y - 0.5
    c = c * y + 1.0
    odd = jnp.bitwise_and(quadrant, 1) == 1
    cos = jnp.where(odd, s, c)
    sin = jnp.where(odd, c, s)
    cos = jnp.where(jnp.bitwise_and(quadrant + 1, 2) == 2, -cos, cos)
    sin = jnp.where(jnp.bitwise_and(quadrant, 2) == 2, -sin, sin)
    return cos, sin


def times(a, b):
    return a[0] * b[0] - a[1] * b[1], a[0] * b[1] + a[1] * b[0]


def plus_minus(a, b):
    cc, ss, cs, sc = a[0] * b[0], a[1] * b[1], a[0] * b[1], a[1] * b[0]
    return (cc - ss, sc + cs), (cc + ss, sc - cs)


def powers(e1):
    e = {1: e1}
    e[2] = times(e1, e1)
    e[3] = times(e[2], e1)
    e[4] = times(e[2], e[2])
    e[8] = times(e[4], e[4])
    e[12], _ = plus_minus(e[8], e[4])
    for d in (1, 2, 3):
        e[8 + d], e[8 - d] = plus_minus(e[8], e[d])
    e[16] = times(e[8], e[8])
    for d in (1, 2, 3):
        _, e[16 - d] = plus_minus(e[16], e[d])
    return e


def prepare(data, slot, first_block, xs, yc, ys, zc, zs, first_w, group, y_waves):
    middle = (group - 1) // 2
    frames = data.shape[2]

    def step(i, _):
        at = pl.ds(pl.multiple_of(i * LANES, LANES), LANES)
        to = first_block + i
        n = data[slot, 0, :, at].astype(jnp.int32)
        xs[to, 0], xs[to, 1] = sincos((first_w + middle) * n)
        e1 = sincos(n)
        e = {1: e1}
        for d in range(2, group - middle):
            e[d] = times(e[d - 1], e1)
        for d in range(1, group - middle):
            xs[to, 2 * d], xs[to, 2 * d + 1] = e[d]
        e = powers(sincos(data[slot, 1, :, at].astype(jnp.int32)))
        for row, w in enumerate(y_waves):
            c, s = e[abs(w)]
            yc[to, row * frames : (row + 1) * frames, :] = c
            ys[to, row * frames : (row + 1) * frames, :] = s if w > 0 else -s
        e = powers(sincos(data[slot, 2, :, at].astype(jnp.int32)))
        for w in range(1, HALF_Z + 1):
            c, s = e[w]
            zc[to, (w - 1) * frames : w * frames, :] = c
            zs[to, (w - 1) * frames : w * frames, :] = s
        return 0

    lax.fori_loop(0, data.shape[3] // LANES, step, 0)


def frame_product(f, data, first_slot, xs, yc, ys, zc, zs, block, group, rows):
    middle = (group - 1) // 2
    frames, lanes = data.shape[2], data.shape[3]
    total = None
    steps = block // LANES

    def wide(get):
        return jnp.concatenate([get(k) for k in range(steps)], 1)

    for i in range(2 * lanes // block):
        first = i * steps
        slot, at = first_slot + i * block // lanes, pl.ds(i * block % lanes, block)

        def pick(ref):
            return wide(lambda k: ref[first + k, pl.ds(f, rows, stride=frames), :])

        y = (pick(yc), pick(ys))
        x = [wide(lambda k: xs[first + k, j, pl.ds(f, 1), :]) for j in range(2 * (group - middle))]
        mid = times((x[0], x[1]), y)
        e = {middle: mid}
        for d in range(1, group - middle):
            up, down = plus_minus(mid, (x[2 * d], x[2 * d + 1]))
            e[middle + d] = up
            if middle - d >= 0:
                e[middle - d] = down
        left = []
        for j in range(group):
            left += [e[j][0].astype(jnp.bfloat16), e[j][1].astype(jnp.bfloat16)]
        left = jnp.concatenate(left, 0)
        right = []
        for z in (pick(zc), pick(zs)):
            right.append(z.astype(jnp.bfloat16))
            for a in range(COMPS - 1):
                right.append((z * data[slot, 3 + a, pl.ds(f, 1), at]).astype(jnp.bfloat16))
        right = jnp.concatenate(right, 0)
        part = lax.dot_general(
            left, right, (((1,), (1,)), ((), ())), preferred_element_type=jnp.float32
        )
        total = part if total is None else total + part
    return total


def combine(raw, group, rows):
    lane = lax.broadcasted_iota(jnp.int32, (rows, LANES), 1)
    sign = jnp.where(lane < LANES // 2, -1.0, 1.0)
    out = []
    for j in range(group):
        re = raw[2 * j * rows : (2 * j + 1) * rows]
        im = raw[(2 * j + 1) * rows : (2 * j + 2) * rows]
        turned = pltpu.roll(im, LANES // 2, 1) * sign
        out.append(jnp.concatenate([re + turned, re - turned], 1))
    return out


def fold_matrices():
    lane = lax.broadcasted_iota(jnp.int32, (LANES, LANES), 0)
    goal = lax.broadcasted_iota(jnp.int32, (LANES, LANES), 1)
    comp = jnp.right_shift(jnp.bitwise_and(lane, 63), 4)
    step = jnp.bitwise_and(lane, HALF_Z - 1)
    own = []
    for qz in (KZ // 2 + step, KZ // 2 - 1 - step):
        own.append(comp * KZ + qz)
    mirror = [comp * KZ + KZ - 1 - (t - comp * KZ) for t in own]
    return [[(goal == t).astype(jnp.float32).astype(jnp.bfloat16) for t in side] for side in (own, mirror)]


def exact_dot(x, matrix):
    high = x.astype(jnp.bfloat16)
    low = (x - high.astype(jnp.float32)).astype(jnp.bfloat16)
    return jnp.dot(high, matrix, preferred_element_type=jnp.float32) + jnp.dot(
        low, matrix, preferred_element_type=jnp.float32
    )


def correlate(series, wide, sums, frames, rows, atoms):
    tall = min(8, rows)
    slots = 2 * (rows // tall)
    anchors = 8

    def widen(t, _):
        block = series(t).astype(jnp.float32)
        for slot in range(slots):
            r, half = divmod(slot, 2)
            wide[slot, t] = block[r * tall : (r + 1) * tall, half * LANES : (half + 1) * LANES]
        return 0

    lax.fori_loop(0, frames, widen, 0)
    for slot in range(slots):
        r, half = divmod(slot, 2)
        for t in range(LAGS):
            wide[slot, frames + t] = jnp.zeros((tall, LANES), jnp.float32)

        def step(i, acc):
            first = i * anchors
            window = [wide[slot, first + t] for t in range(LAGS)]
            for t in range(anchors):
                acc = tuple(acc[lag] + window[0] * window[lag] for lag in range(LAGS))
                window = window[1:]
                if t < anchors - 1:
                    window.append(wide[slot, first + t + LAGS])
            return acc

        zero = jnp.zeros((tall, LANES), jnp.float32)
        acc = lax.fori_loop(0, frames // anchors, step, (zero,) * LAGS)
        for lag in range(LAGS):
            sums[half, lag * rows + r * tall : lag * rows + (r + 1) * tall, :] = acc[lag] * (
                1.0 / (atoms * (frames - lag))
            )


def arrange(sums, folded, fold, out_ref, first_lane, rows, flip):
    groups = max(1, rows // 4)
    per = rows // groups
    lane = lax.broadcasted_iota(jnp.int32, (LAGS, LANES), 1)
    block = jnp.right_shift(lane, 5)
    folded[...] = exact_dot(sums[0], fold[0]) + exact_dot(sums[1], fold[1])
    for g in range(groups):
        parts = [folded[pl.ds(g * per + i, LAGS, stride=rows), :] for i in range(per)]
        if flip:
            parts = parts[::-1]
        goal = first_lane + (groups - 1 - g if flip else g) * LANES
        for c in range(COMPS):
            out = jnp.zeros((LAGS, LANES), jnp.float32)
            for i in range(per):
                shift = ((i - c) * KZ) % LANES
                part = parts[i] if shift == 0 else pltpu.roll(parts[i], shift, 1)
                out = jnp.where(block == i, part, out)
            out_ref[c, :, goal : goal + LANES] = out


def kernel(
    dims, data_ref, out_ref, data, xs, yc, ys, zc, zs, total, stage, series, wide, sums, folded,
    mirror, in_recv, x_send, relay_send, mode_send, mode_recv, mirror_send, mirror_recv,
):
    atom_ways, time_ways, y_waves, atoms = dims
    frames = data.shape[2]
    group = KX // atom_ways
    rows = KY // 2
    owned = stage.shape[2]
    split = rows // owned
    chips = atom_ways // 2
    a, t = lax.axis_index("atom"), lax.axis_index("tm")
    chip, core = a // 2, a % 2
    first = a * group
    first_w = first - KX // 2 + (first >= KX // 2).astype(jnp.int32)

    mate = (chip * 2 + 1 - core, t)
    opposite = (atom_ways - 1 - a, time_ways - 1 - t)

    def along_x(step):
        return (((chip + step) % chips) * 2 + core, t)

    def along_time(step):
        return (t + step) % time_ways

    def signal(device):
        pl.semaphore_signal(
            pltpu.get_barrier_semaphore(), inc=1, device_id=device, device_id_type=pl.DeviceIdType.MESH
        )

    def remote(src, dst, send, recv, device):
        return pltpu.make_async_remote_copy(
            src_ref=src, dst_ref=dst, send_sem=send, recv_sem=recv, device_id=device,
            device_id_type=pl.DeviceIdType.MESH,
        )

    signal(mate)
    signal(opposite)
    for step in range(1, chips):
        signal(along_x(step))
    for step in range(1, time_ways):
        signal((a, along_time(step)))

    data[0] = data_ref[...]
    total[...] = jnp.zeros_like(total)
    pl.semaphore_wait(pltpu.get_barrier_semaphore(), chips + time_ways)

    def shipped(step):
        return remote(data.at[0], data.at[2 * step], x_send.at[step], in_recv.at[2 * step], along_x(step))

    def relayed(p):
        return remote(
            data.at[2 * p], data.at[2 * p + 1], relay_send.at[p], in_recv.at[2 * p + 1], mate
        )

    def mode_copy(step, f):
        goal = along_time(step)
        return remote(
            stage.at[goal, f], series.at[t, f], mode_send.at[step, f], mode_recv.at[step, f], (a, goal)
        )

    for step in range(1, chips):
        shipped(step).start()

    def phase(p, _):
        @pl.when(p > 0)
        def _():
            shipped(p).wait_recv()

        relayed(p).start()
        prepare(data, 2 * p, 0, xs, yc, ys, zc, zs, first_w, group, y_waves)
        relayed(p).wait_recv()
        prepare(data, 2 * p + 1, data.shape[3] // LANES, xs, yc, ys, zc, zs, first_w, group, y_waves)

        def frame_step(f, _):
            total[f] += frame_product(f, data, 2 * p, xs, yc, ys, zc, zs, 4 * LANES, group, rows)

            @pl.when(p == chips - 1)
            def _():
                for j, block in enumerate(combine(total[f], group, rows)):
                    block = block.astype(stage.dtype)
                    for k in range(split):
                        stage[j * split + k, f] = block[k * owned : (k + 1) * owned]
                series[t, f] = stage[t, f]
                for step in range(1, time_ways):
                    mode_copy(step, f).start()

            return 0

        lax.fori_loop(0, frames, frame_step, 0)
        return 0

    lax.fori_loop(0, chips, phase, 0)

    def arrived(f, _):
        for step in range(1, time_ways):
            mode_copy(step, f).wait_recv()
        return 0

    lax.fori_loop(0, frames, arrived, 0)
    correlate(
        lambda u: series[u // frames, u % frames], wide, sums, time_ways * frames, owned, atoms
    )
    own_fold, mirror_fold = fold_matrices()
    arrange(sums, folded, mirror_fold, mirror, 0, owned, True)
    half = owned * KZ
    swap = remote(mirror, out_ref.at[:, :, pl.ds(0, half)], mirror_send, mirror_recv, opposite)
    swap.start()
    arrange(sums, folded, own_fold, out_ref, half, owned, False)

    def sent(f, _):
        for step in range(1, time_ways):
            mode_copy(step, f).wait_send()
        return 0

    lax.fori_loop(0, frames, sent, 0)
    for step in range(1, chips):
        shipped(step).wait_send()
    for p in range(chips):
        relayed(p).wait_send()
    swap.wait()


def call(data, atom_ways, time_ways, rows, y_waves):
    frames, lanes = data.shape[1], data.shape[2]
    atoms = lanes * atom_ways
    group = KX // atom_ways
    blocks = 2 * lanes // LANES
    tall = min(8, rows)
    dims = (atom_ways, time_ways, y_waves, atoms)
    whole = pl.BlockSpec(memory_space=pltpu.VMEM)
    dma = pltpu.SemaphoreType.DMA
    tabled = pltpu.VMEM((blocks, KY // 2 * frames, LANES), jnp.float32)
    return pl.pallas_call(
        functools.partial(kernel, dims),
        out_shape=jax.ShapeDtypeStruct((COMPS, LAGS, 2 * rows * KZ), jnp.float32),
        in_specs=[whole],
        out_specs=whole,
        scratch_shapes=[
            pltpu.VMEM((atom_ways,) + data.shape, jnp.float32),
            pltpu.VMEM((blocks, 2 * (group - (group - 1) // 2), frames, LANES), jnp.float32),
            tabled, tabled, tabled, tabled,
            pltpu.VMEM((frames, group * KY, LANES), jnp.float32),
            pltpu.VMEM((time_ways, frames, rows, 2 * LANES), WIRE),
            pltpu.VMEM((time_ways, frames, rows, 2 * LANES), WIRE),
            pltpu.VMEM((2 * (rows // tall), time_ways * frames + LAGS, tall, LANES), jnp.float32),
            pltpu.VMEM((2, LAGS * rows, LANES), jnp.float32),
            pltpu.VMEM((LAGS * rows, LANES), jnp.float32),
            pltpu.VMEM((COMPS, LAGS, rows * KZ), jnp.float32),
            dma((atom_ways,)),
            dma((atom_ways // 2,)),
            dma((atom_ways // 2,)),
            dma((time_ways, frames)),
            dma((time_ways, frames)),
            dma,
            dma,
        ],
        compiler_params=pltpu.CompilerParams(
            vmem_limit_bytes=VMEM, collective_id=0, has_side_effects=True
        ),
        name="factors",
    )(data)


def per_device(positions, velocity):
    atom_ways = lax.axis_size("atom")
    time_ways = lax.axis_size("tm")
    owned = KX * KY // (atom_ways * time_ways)
    rows = owned // 2
    y_waves = [wave(q, KY) for q in range(KY) if q % owned >= rows]
    data = jnp.concatenate([positions.astype(jnp.float32), velocity.astype(jnp.float32)], 1)
    return call(jnp.transpose(data, (1, 0, 2)), atom_ways, time_ways, rows, y_waves)


def solution(mesh):
    in_specs = (P("tm", None, "atom"), P("tm", None, "atom"))
    out_specs = P(None, None, ("atom", "tm"))
    return jax.shard_map(
        per_device, mesh=mesh, in_specs=in_specs, out_specs=out_specs, check_vma=False
    )
```

```python
import functools
import math

import jax
import jax.numpy as jnp
from jax import lax
from jax.experimental import pallas as pl
from jax.experimental.pallas import tpu as pltpu
from jax.sharding import PartitionSpec as P

KX = 32
KY = 32
KZ = 32
LAGS = 16
LATTICE = 131072
QUARTER = LATTICE // 4
HALF_Z = KZ // 2
COMPS = 4
LANES = 128
VMEM = 56 * 1024 * 1024
WIRE = jnp.bfloat16


def wave(q, extent):
    return q - extent // 2 + (1 if q >= extent // 2 else 0)


def sincos(n):
    n = jnp.bitwise_and(n, LATTICE - 1)
    quadrant = jnp.right_shift(n + QUARTER // 2, 15)
    x = (n - jnp.left_shift(quadrant, 15)).astype(jnp.float32) * (2.0 * math.pi / LATTICE)
    y = x * x
    s = y * (1.0 / 362880.0) - 1.0 / 5040.0
    s = s * y + 1.0 / 120.0
    s = s * y - 1.0 / 6.0
    s = s * y * x + x
    c = y * (1.0 / 40320.0) - 1.0 / 720.0
    c = c * y + 1.0 / 24.0
    c = c * y - 0.5
    c = c * y + 1.0
    odd = jnp.bitwise_and(quadrant, 1) == 1
    cos = jnp.where(odd, s, c)
    sin = jnp.where(odd, c, s)
    cos = jnp.where(jnp.bitwise_and(quadrant + 1, 2) == 2, -cos, cos)
    sin = jnp.where(jnp.bitwise_and(quadrant, 2) == 2, -sin, sin)
    return cos, sin


def times(a, b):
    return a[0] * b[0] - a[1] * b[1], a[0] * b[1] + a[1] * b[0]


def plus_minus(a, b):
    cc, ss, cs, sc = a[0] * b[0], a[1] * b[1], a[0] * b[1], a[1] * b[0]
    return (cc - ss, sc + cs), (cc + ss, sc - cs)


def powers(e1):
    e = {1: e1}
    e[2] = times(e1, e1)
    e[3] = times(e[2], e1)
    e[4] = times(e[2], e[2])
    e[8] = times(e[4], e[4])
    e[12], _ = plus_minus(e[8], e[4])
    for d in (1, 2, 3):
        e[8 + d], e[8 - d] = plus_minus(e[8], e[d])
    e[16] = times(e[8], e[8])
    for d in (1, 2, 3):
        _, e[16 - d] = plus_minus(e[16], e[d])
    return e


def prepare(data, slot, first_block, xs, yc, ys, zc, zs, first_w, group, y_waves):
    middle = (group - 1) // 2
    frames = data.shape[2]

    def step(i, _):
        at = pl.ds(pl.multiple_of(i * LANES, LANES), LANES)
        to = first_block + i
        n = data[slot, 0, :, at].astype(jnp.int32)
        xs[to, 0], xs[to, 1] = sincos((first_w + middle) * n)
        e1 = sincos(n)
        e = {1: e1}
        for d in range(2, group - middle):
            e[d] = times(e[d - 1], e1)
        for d in range(1, group - middle):
            xs[to, 2 * d], xs[to, 2 * d + 1] = e[d]
        e = powers(sincos(data[slot, 1, :, at].astype(jnp.int32)))
        for row, w in enumerate(y_waves):
            c, s = e[abs(w)]
            yc[to, row * frames : (row + 1) * frames, :] = c
            ys[to, row * frames : (row + 1) * frames, :] = s if w > 0 else -s
        e = powers(sincos(data[slot, 2, :, at].astype(jnp.int32)))
        for w in range(1, HALF_Z + 1):
            c, s = e[w]
            zc[to, (w - 1) * frames : w * frames, :] = c
            zs[to, (w - 1) * frames : w * frames, :] = s
        return 0

    lax.fori_loop(0, data.shape[3] // LANES, step, 0)


def frame_product(f, data, first_slot, xs, yc, ys, zc, zs, block, group, rows):
    middle = (group - 1) // 2
    frames, lanes = data.shape[2], data.shape[3]
    total = None
    steps = block // LANES

    def wide(get):
        return jnp.concatenate([get(k) for k in range(steps)], 1)

    for i in range(2 * lanes // block):
        first = i * steps
        slot, at = first_slot + i * block // lanes, pl.ds(i * block % lanes, block)

        def pick(ref):
            return wide(lambda k: ref[first + k, pl.ds(f, rows, stride=frames), :])

        y = (pick(yc), pick(ys))
        x = [wide(lambda k: xs[first + k, j, pl.ds(f, 1), :]) for j in range(2 * (group - middle))]
        mid = times((x[0], x[1]), y)
        e = {middle: mid}
        for d in range(1, group - middle):
            up, down = plus_minus(mid, (x[2 * d], x[2 * d + 1]))
            e[middle + d] = up
            if middle - d >= 0:
                e[middle - d] = down
        left = []
        for j in range(group):
            left += [e[j][0].astype(jnp.bfloat16), e[j][1].astype(jnp.bfloat16)]
        left = jnp.concatenate(left, 0)
        right = []
        for z in (pick(zc), pick(zs)):
            right.append(z.astype(jnp.bfloat16))
            for a in range(COMPS - 1):
                right.append((z * data[slot, 3 + a, pl.ds(f, 1), at]).astype(jnp.bfloat16))
        right = jnp.concatenate(right, 0)
        part = lax.dot_general(
            right, left, (((1,), (1,)), ((), ())), preferred_element_type=jnp.float32
        )
        total = part if total is None else total + part
    return total


def combine(raw, group, rows):
    lane = lax.broadcasted_iota(jnp.int32, (rows, LANES), 1)
    sign = jnp.where(lane < LANES // 2, -1.0, 1.0)
    out = []
    for j in range(group):
        re = raw[2 * j * rows : (2 * j + 1) * rows]
        im = raw[(2 * j + 1) * rows : (2 * j + 2) * rows]
        turned = pltpu.roll(im, LANES // 2, 1) * sign
        out.append(jnp.concatenate([re + turned, re - turned], 1))
    return out


def fold_matrices():
    lane = lax.broadcasted_iota(jnp.int32, (LANES, LANES), 0)
    goal = lax.broadcasted_iota(jnp.int32, (LANES, LANES), 1)
    comp = jnp.right_shift(jnp.bitwise_and(lane, 63), 4)
    step = jnp.bitwise_and(lane, HALF_Z - 1)
    own = []
    for qz in (KZ // 2 + step, KZ // 2 - 1 - step):
        own.append(comp * KZ + qz)
    mirror = [comp * KZ + KZ - 1 - (t - comp * KZ) for t in own]
    return [[(goal == t).astype(jnp.float32).astype(jnp.bfloat16) for t in side] for side in (own, mirror)]


def exact_dot(x, matrix):
    high = x.astype(jnp.bfloat16)
    low = (x - high.astype(jnp.float32)).astype(jnp.bfloat16)
    return jnp.dot(high, matrix, preferred_element_type=jnp.float32) + jnp.dot(
        low, matrix, preferred_element_type=jnp.float32
    )


def correlate(series, wide, sums, frames, rows, atoms):
    tall = min(8, rows)
    slots = 2 * (rows // tall)
    anchors = 8

    def widen(t, _):
        block = series(t).astype(jnp.float32)
        for slot in range(slots):
            r, half = divmod(slot, 2)
            wide[slot, t] = block[r * tall : (r + 1) * tall, half * LANES : (half + 1) * LANES]
        return 0

    lax.fori_loop(0, frames, widen, 0)
    for slot in range(slots):
        r, half = divmod(slot, 2)
        for t in range(LAGS):
            wide[slot, frames + t] = jnp.zeros((tall, LANES), jnp.float32)

        def step(i, acc):
            first = i * anchors
            window = [wide[slot, first + t] for t in range(LAGS)]
            for t in range(anchors):
                acc = tuple(acc[lag] + window[0] * window[lag] for lag in range(LAGS))
                window = window[1:]
                if t < anchors - 1:
                    window.append(wide[slot, first + t + LAGS])
            return acc

        zero = jnp.zeros((tall, LANES), jnp.float32)
        acc = lax.fori_loop(0, frames // anchors, step, (zero,) * LAGS)
        for lag in range(LAGS):
            sums[half, lag * rows + r * tall : lag * rows + (r + 1) * tall, :] = acc[lag] * (
                1.0 / (atoms * (frames - lag))
            )


def arrange(sums, folded, fold, out_ref, first_lane, rows, flip):
    groups = max(1, rows // 4)
    per = rows // groups
    lane = lax.broadcasted_iota(jnp.int32, (LAGS, LANES), 1)
    block = jnp.right_shift(lane, 5)
    folded[...] = exact_dot(sums[0], fold[0]) + exact_dot(sums[1], fold[1])
    for g in range(groups):
        parts = [folded[pl.ds(g * per + i, LAGS, stride=rows), :] for i in range(per)]
        if flip:
            parts = parts[::-1]
        goal = first_lane + (groups - 1 - g if flip else g) * LANES
        for c in range(COMPS):
            out = jnp.zeros((LAGS, LANES), jnp.float32)
            for i in range(per):
                shift = ((i - c) * KZ) % LANES
                part = parts[i] if shift == 0 else pltpu.roll(parts[i], shift, 1)
                out = jnp.where(block == i, part, out)
            out_ref[c, :, goal : goal + LANES] = out


def kernel(
    dims, data_ref, out_ref, data, xs, yc, ys, zc, zs, total, stage, series, wide, sums, folded,
    mirror, in_recv, x_send, relay_send, mode_send, mode_recv, mirror_send, mirror_recv,
):
    atom_ways, time_ways, y_waves, atoms = dims
    frames = data.shape[2]
    group = KX // atom_ways
    rows = KY // 2
    owned = stage.shape[2]
    split = rows // owned
    chips = atom_ways // 2
    a, t = lax.axis_index("atom"), lax.axis_index("tm")
    chip, core = a // 2, a % 2
    first = a * group
    first_w = first - KX // 2 + (first >= KX // 2).astype(jnp.int32)

    mate = (chip * 2 + 1 - core, t)
    opposite = (atom_ways - 1 - a, time_ways - 1 - t)

    def along_x(step):
        return (((chip + step) % chips) * 2 + core, t)

    def along_time(step):
        return (t + step) % time_ways

    def signal(device):
        pl.semaphore_signal(
            pltpu.get_barrier_semaphore(), inc=1, device_id=device, device_id_type=pl.DeviceIdType.MESH
        )

    def remote(src, dst, send, recv, device):
        return pltpu.make_async_remote_copy(
            src_ref=src, dst_ref=dst, send_sem=send, recv_sem=recv, device_id=device,
            device_id_type=pl.DeviceIdType.MESH,
        )

    signal(mate)
    signal(opposite)
    for step in range(1, chips):
        signal(along_x(step))
    for step in range(1, time_ways):
        signal((a, along_time(step)))

    data[0] = data_ref[...]
    total[...] = jnp.zeros_like(total)
    pl.semaphore_wait(pltpu.get_barrier_semaphore(), chips + time_ways)

    def shipped(step):
        return remote(data.at[0], data.at[2 * step], x_send.at[step], in_recv.at[2 * step], along_x(step))

    def relayed(p):
        return remote(
            data.at[2 * p], data.at[2 * p + 1], relay_send.at[p], in_recv.at[2 * p + 1], mate
        )

    def mode_copy(step, f):
        goal = along_time(step)
        return remote(
            stage.at[goal, f], series.at[t, f], mode_send.at[step, f], mode_recv.at[step, f], (a, goal)
        )

    for step in range(1, chips):
        shipped(step).start()

    def phase(p, _):
        @pl.when(p > 0)
        def _():
            shipped(p).wait_recv()

        relayed(p).start()
        prepare(data, 2 * p, 0, xs, yc, ys, zc, zs, first_w, group, y_waves)
        relayed(p).wait_recv()
        prepare(data, 2 * p + 1, data.shape[3] // LANES, xs, yc, ys, zc, zs, first_w, group, y_waves)

        def frame_step(f, _):
            total[f] += frame_product(f, data, 2 * p, xs, yc, ys, zc, zs, 4 * LANES, group, rows)

            @pl.when(p == chips - 1)
            def _():
                for j, block in enumerate(combine(jnp.transpose(total[f]), group, rows)):
                    block = block.astype(stage.dtype)
                    for k in range(split):
                        stage[j * split + k, f] = block[k * owned : (k + 1) * owned]
                series[t, f] = stage[t, f]
                for step in range(1, time_ways):
                    mode_copy(step, f).start()

            return 0

        lax.fori_loop(0, frames, frame_step, 0)
        return 0

    lax.fori_loop(0, chips, phase, 0)

    def arrived(f, _):
        for step in range(1, time_ways):
            mode_copy(step, f).wait_recv()
        return 0

    lax.fori_loop(0, frames, arrived, 0)
    correlate(
        lambda u: series[u // frames, u % frames], wide, sums, time_ways * frames, owned, atoms
    )
    own_fold, mirror_fold = fold_matrices()
    arrange(sums, folded, mirror_fold, mirror, 0, owned, True)
    half = owned * KZ
    swap = remote(mirror, out_ref.at[:, :, pl.ds(0, half)], mirror_send, mirror_recv, opposite)
    swap.start()
    arrange(sums, folded, own_fold, out_ref, half, owned, False)

    def sent(f, _):
        for step in range(1, time_ways):
            mode_copy(step, f).wait_send()
        return 0

    lax.fori_loop(0, frames, sent, 0)
    for step in range(1, chips):
        shipped(step).wait_send()
    for p in range(chips):
        relayed(p).wait_send()
    swap.wait()


def call(data, atom_ways, time_ways, rows, y_waves):
    frames, lanes = data.shape[1], data.shape[2]
    atoms = lanes * atom_ways
    group = KX // atom_ways
    blocks = 2 * lanes // LANES
    tall = min(8, rows)
    dims = (atom_ways, time_ways, y_waves, atoms)
    whole = pl.BlockSpec(memory_space=pltpu.VMEM)
    dma = pltpu.SemaphoreType.DMA
    tabled = pltpu.VMEM((blocks, KY // 2 * frames, LANES), jnp.float32)
    return pl.pallas_call(
        functools.partial(kernel, dims),
        out_shape=jax.ShapeDtypeStruct((COMPS, LAGS, 2 * rows * KZ), jnp.float32),
        in_specs=[whole],
        out_specs=whole,
        scratch_shapes=[
            pltpu.VMEM((atom_ways,) + data.shape, jnp.float32),
            pltpu.VMEM((blocks, 2 * (group - (group - 1) // 2), frames, LANES), jnp.float32),
            tabled, tabled, tabled, tabled,
            pltpu.VMEM((frames, LANES, group * KY), jnp.float32),
            pltpu.VMEM((time_ways, frames, rows, 2 * LANES), WIRE),
            pltpu.VMEM((time_ways, frames, rows, 2 * LANES), WIRE),
            pltpu.VMEM((2 * (rows // tall), time_ways * frames + LAGS, tall, LANES), jnp.float32),
            pltpu.VMEM((2, LAGS * rows, LANES), jnp.float32),
            pltpu.VMEM((LAGS * rows, LANES), jnp.float32),
            pltpu.VMEM((COMPS, LAGS, rows * KZ), jnp.float32),
            dma((atom_ways,)),
            dma((atom_ways // 2,)),
            dma((atom_ways // 2,)),
            dma((time_ways, frames)),
            dma((time_ways, frames)),
            dma,
            dma,
        ],
        compiler_params=pltpu.CompilerParams(
            vmem_limit_bytes=VMEM, collective_id=0, has_side_effects=True
        ),
        name="factors",
    )(data)


def per_device(positions, velocity):
    atom_ways = lax.axis_size("atom")
    time_ways = lax.axis_size("tm")
    owned = KX * KY // (atom_ways * time_ways)
    rows = owned // 2
    y_waves = [wave(q, KY) for q in range(KY) if q % owned >= rows]
    data = jnp.concatenate([positions.astype(jnp.float32), velocity.astype(jnp.float32)], 1)
    return call(jnp.transpose(data, (1, 0, 2)), atom_ways, time_ways, rows, y_waves)


def solution(mesh):
    in_specs = (P("tm", None, "atom"), P("tm", None, "atom"))
    out_specs = P(None, None, ("atom", "tm"))
    return jax.shard_map(
        per_device, mesh=mesh, in_specs=in_specs, out_specs=out_specs, check_vma=False
    )
```

```python
import functools
import math

import jax
import jax.numpy as jnp
from jax import lax
from jax.experimental import pallas as pl
from jax.experimental.pallas import tpu as pltpu
from jax.sharding import PartitionSpec as P

KX = 32
KY = 32
KZ = 32
LAGS = 16
LATTICE = 131072
QUARTER = LATTICE // 4
HALF_Z = KZ // 2
COMPS = 4
LANES = 128
VMEM = 56 * 1024 * 1024
WIRE = jnp.bfloat16


def wave(q, extent):
    return q - extent // 2 + (1 if q >= extent // 2 else 0)


def sincos(n):
    n = jnp.bitwise_and(n, LATTICE - 1)
    quadrant = jnp.right_shift(n + QUARTER // 2, 15)
    x = (n - jnp.left_shift(quadrant, 15)).astype(jnp.float32) * (2.0 * math.pi / LATTICE)
    y = x * x
    s = y * (1.0 / 362880.0) - 1.0 / 5040.0
    s = s * y + 1.0 / 120.0
    s = s * y - 1.0 / 6.0
    s = s * y * x + x
    c = y * (1.0 / 40320.0) - 1.0 / 720.0
    c = c * y + 1.0 / 24.0
    c = c * y - 0.5
    c = c * y + 1.0
    odd = jnp.bitwise_and(quadrant, 1) == 1
    cos = jnp.where(odd, s, c)
    sin = jnp.where(odd, c, s)
    cos = jnp.where(jnp.bitwise_and(quadrant + 1, 2) == 2, -cos, cos)
    sin = jnp.where(jnp.bitwise_and(quadrant, 2) == 2, -sin, sin)
    return cos, sin


def times(a, b):
    return a[0] * b[0] - a[1] * b[1], a[0] * b[1] + a[1] * b[0]


def plus_minus(a, b):
    cc, ss, cs, sc = a[0] * b[0], a[1] * b[1], a[0] * b[1], a[1] * b[0]
    return (cc - ss, sc + cs), (cc + ss, sc - cs)


def powers(e1):
    e = {1: e1}
    e[2] = times(e1, e1)
    e[3] = times(e[2], e1)
    e[4] = times(e[2], e[2])
    e[8] = times(e[4], e[4])
    e[12], _ = plus_minus(e[8], e[4])
    for d in (1, 2, 3):
        e[8 + d], e[8 - d] = plus_minus(e[8], e[d])
    e[16] = times(e[8], e[8])
    for d in (1, 2, 3):
        _, e[16 - d] = plus_minus(e[16], e[d])
    return e


def prepare(data, slot, first_block, xs, yc, ys, zc, zs, first_w, group, y_waves):
    middle = (group - 1) // 2
    frames = data.shape[2]

    def block(i):
        at = pl.ds(pl.multiple_of(i * LANES, LANES), LANES)
        to = first_block + i
        n = data[slot, 0, :, at].astype(jnp.int32)
        xs[to, 0], xs[to, 1] = sincos((first_w + middle) * n)
        e1 = sincos(n)
        e = {1: e1}
        for d in range(2, group - middle):
            e[d] = times(e[d - 1], e1)
        for d in range(1, group - middle):
            xs[to, 2 * d], xs[to, 2 * d + 1] = e[d]
        e = powers(sincos(data[slot, 1, :, at].astype(jnp.int32)))
        for row, w in enumerate(y_waves):
            c, s = e[abs(w)]
            yc[to, row * frames : (row + 1) * frames, :] = c
            ys[to, row * frames : (row + 1) * frames, :] = s if w > 0 else -s
        e = powers(sincos(data[slot, 2, :, at].astype(jnp.int32)))
        for w in range(1, HALF_Z + 1):
            c, s = e[w]
            zc[to, (w - 1) * frames : w * frames, :] = c
            zs[to, (w - 1) * frames : w * frames, :] = s

    def step(i, _):
        block(2 * i)
        block(2 * i + 1)
        return 0

    lax.fori_loop(0, data.shape[3] // (2 * LANES), step, 0)


def frame_product(f, data, p, xs, yc, ys, zc, zs, block, group, rows):
    middle = (group - 1) // 2
    frames, lanes = data.shape[2], data.shape[3]
    total = None
    steps = block // LANES

    def wide(get):
        return jnp.concatenate([get(k) for k in range(steps)], 1)

    for i in range(2 * lanes // block):
        first = p * (2 * lanes // LANES) + i * steps
        slot, at = 2 * p + i * block // lanes, pl.ds(i * block % lanes, block)

        def pick(ref):
            return wide(lambda k: ref[first + k, pl.ds(f, rows, stride=frames), :])

        y = (pick(yc), pick(ys))
        x = [wide(lambda k: xs[first + k, j, pl.ds(f, 1), :]) for j in range(2 * (group - middle))]
        mid = times((x[0], x[1]), y)
        e = {middle: mid}
        for d in range(1, group - middle):
            up, down = plus_minus(mid, (x[2 * d], x[2 * d + 1]))
            e[middle + d] = up
            if middle - d >= 0:
                e[middle - d] = down
        left = []
        for j in range(group):
            left += [e[j][0].astype(jnp.bfloat16), e[j][1].astype(jnp.bfloat16)]
        left = jnp.concatenate(left, 0)
        right = []
        for z in (pick(zc), pick(zs)):
            right.append(z.astype(jnp.bfloat16))
            for a in range(COMPS - 1):
                right.append((z * data[slot, 3 + a, pl.ds(f, 1), at]).astype(jnp.bfloat16))
        right = jnp.concatenate(right, 0)
        part = lax.dot_general(
            right, left, (((1,), (1,)), ((), ())), preferred_element_type=jnp.float32
        )
        total = part if total is None else total + part
    return total


def combine(raw, group, rows):
    lane = lax.broadcasted_iota(jnp.int32, (rows, LANES), 1)
    sign = jnp.where(lane < LANES // 2, -1.0, 1.0)
    out = []
    for j in range(group):
        re = raw[2 * j * rows : (2 * j + 1) * rows]
        im = raw[(2 * j + 1) * rows : (2 * j + 2) * rows]
        turned = pltpu.roll(im, LANES // 2, 1) * sign
        out.append(jnp.concatenate([re + turned, re - turned], 1))
    return out


def fold_matrices():
    lane = lax.broadcasted_iota(jnp.int32, (LANES, LANES), 0)
    goal = lax.broadcasted_iota(jnp.int32, (LANES, LANES), 1)
    comp = jnp.right_shift(jnp.bitwise_and(lane, 63), 4)
    step = jnp.bitwise_and(lane, HALF_Z - 1)
    own = []
    for qz in (KZ // 2 + step, KZ // 2 - 1 - step):
        own.append(comp * KZ + qz)
    mirror = [comp * KZ + KZ - 1 - (t - comp * KZ) for t in own]
    return [[(goal == t).astype(jnp.float32).astype(jnp.bfloat16) for t in side] for side in (own, mirror)]


def exact_dot(x, matrix):
    high = x.astype(jnp.bfloat16)
    low = (x - high.astype(jnp.float32)).astype(jnp.bfloat16)
    return jnp.dot(high, matrix, preferred_element_type=jnp.float32) + jnp.dot(
        low, matrix, preferred_element_type=jnp.float32
    )


def widen(series, source, wide):
    frames, rows = series.shape[1], series.shape[2]
    tall = min(8, rows)
    for f in range(frames):
        block = series[source, f].astype(jnp.float32)
        for slot in range(wide.shape[0]):
            r, half = divmod(slot, 2)
            wide[slot, source * frames + f] = block[
                r * tall : (r + 1) * tall, half * LANES : (half + 1) * LANES
            ]


def correlate(wide, sums, r, frames, tall, atoms):
    anchors = 8
    for half in range(2):
        slot = 2 * r + half

        def step(i, acc):
            first = i * anchors
            window = [wide[slot, first + t] for t in range(LAGS)]
            for t in range(anchors):
                acc = tuple(acc[lag] + window[0] * window[lag] for lag in range(LAGS))
                window = window[1:]
                if t < anchors - 1:
                    window.append(wide[slot, first + t + LAGS])
            return acc

        zero = jnp.zeros((tall, LANES), jnp.float32)
        acc = lax.fori_loop(0, frames // anchors, step, (zero,) * LAGS)
        for lag in range(LAGS):
            sums[half, lag * tall : (lag + 1) * tall, :] = acc[lag] * (1.0 / (atoms * (frames - lag)))


def arrange(sums, folded, fold, out_ref, first_lane, rows, flip):
    groups = max(1, rows // 4)
    per = rows // groups
    lane = lax.broadcasted_iota(jnp.int32, (LAGS, LANES), 1)
    block = jnp.right_shift(lane, 5)
    folded[...] = exact_dot(sums[0], fold[0]) + exact_dot(sums[1], fold[1])
    for g in range(groups):
        parts = [folded[pl.ds(g * per + i, LAGS, stride=rows), :] for i in range(per)]
        if flip:
            parts = parts[::-1]
        goal = first_lane + (groups - 1 - g if flip else g) * LANES
        for c in range(COMPS):
            out = jnp.zeros((LAGS, LANES), jnp.float32)
            for i in range(per):
                shift = ((i - c) * KZ) % LANES
                part = parts[i] if shift == 0 else pltpu.roll(parts[i], shift, 1)
                out = jnp.where(block == i, part, out)
            out_ref[c, :, goal : goal + LANES] = out


def kernel(
    dims, data_ref, out_ref, data, xs, yc, ys, zc, zs, total, stage, series, wide, sums, folded,
    mirror, in_recv, x_send, relay_send, mode_send, mode_recv, mirror_send, mirror_recv,
):
    atom_ways, time_ways, y_waves, atoms = dims
    frames = data.shape[2]
    group = KX // atom_ways
    rows = KY // 2
    owned = stage.shape[2]
    split = rows // owned
    chips = atom_ways // 2
    a, t = lax.axis_index("atom"), lax.axis_index("tm")
    chip, core = a // 2, a % 2
    first = a * group
    first_w = first - KX // 2 + (first >= KX // 2).astype(jnp.int32)

    mate = (chip * 2 + 1 - core, t)
    opposite = (atom_ways - 1 - a, time_ways - 1 - t)

    def along_x(step):
        return (((chip + step) % chips) * 2 + core, t)

    def along_time(step):
        return (t + step) % time_ways

    def signal(device):
        pl.semaphore_signal(
            pltpu.get_barrier_semaphore(), inc=1, device_id=device, device_id_type=pl.DeviceIdType.MESH
        )

    def remote(src, dst, send, recv, device):
        return pltpu.make_async_remote_copy(
            src_ref=src, dst_ref=dst, send_sem=send, recv_sem=recv, device_id=device,
            device_id_type=pl.DeviceIdType.MESH,
        )

    signal(mate)
    signal(opposite)
    for step in range(1, chips):
        signal(along_x(step))
    for step in range(1, time_ways):
        signal((a, along_time(step)))

    data[0] = data_ref[...]
    for slot in range(wide.shape[0]):
        for lag in range(LAGS):
            wide[slot, time_ways * frames + lag] = jnp.zeros(wide.shape[2:], jnp.float32)
    pl.semaphore_wait(pltpu.get_barrier_semaphore(), chips + time_ways)

    def shipped(step):
        return remote(data.at[0], data.at[2 * step], x_send.at[step], in_recv.at[2 * step], along_x(step))

    def relayed(p):
        return remote(
            data.at[2 * p], data.at[2 * p + 1], relay_send.at[p], in_recv.at[2 * p + 1], mate
        )

    def mode_copy(step, f, count):
        goal, at = along_time(step), pl.ds(f, count)
        return remote(
            stage.at[goal, at], series.at[t, at], mode_send.at[step], mode_recv.at[step], (a, goal)
        )

    def mode_arrival(step):
        source = (t + time_ways - step) % time_ways
        return remote(
            stage.at[source], series.at[source], mode_send.at[step], mode_recv.at[step], (a, source)
        )

    for step in range(1, chips):
        shipped(step).start()

    blocks = data.shape[3] // LANES

    def tables(p):
        if p > 0:
            shipped(p).wait_recv()
        relayed(p).start()
        prepare(data, 2 * p, 2 * p * blocks, xs, yc, ys, zc, zs, first_w, group, y_waves)
        relayed(p).wait_recv()
        prepare(data, 2 * p + 1, (2 * p + 1) * blocks, xs, yc, ys, zc, zs, first_w, group, y_waves)

    def product(f, p):
        return frame_product(f, data, p, xs, yc, ys, zc, zs, 4 * LANES, group, rows)

    def emit(f):
        for j, block in enumerate(combine(jnp.transpose(total[f]), group, rows)):
            block = block.astype(stage.dtype)
            for k in range(split):
                stage[j * split + k, f] = block[k * owned : (k + 1) * owned]
        series[t, f] = stage[t, f]
        for step in range(1, time_ways):
            mode_copy(step, f, 1).start()

    early = frames * 5 // 8

    def own_part(f, _):
        total[f] = product(f, 0)
        return 0

    tables(0)
    lax.fori_loop(0, early, own_part, 0)
    for p in range(1, chips):
        tables(p)

        def far_part(f, _):
            total[f] += product(f, p)
            if p == chips - 1:
                emit(f)
            return 0

        lax.fori_loop(0, early, far_part, 0)

    def whole_frame(f, _):
        total[f] = jnp.zeros(total.shape[1:], jnp.float32)

        def part(p, _):
            total[f] += product(f, p)
            return 0

        lax.fori_loop(0, chips, part, 0)
        emit(f)
        return 0

    lax.fori_loop(early, frames, whole_frame, 0)

    widen(series, t, wide)
    for step in range(1, time_ways):
        mode_arrival(step).wait_recv()
        widen(series, (t + time_ways - step) % time_ways, wide)

    own_fold, mirror_fold = fold_matrices()
    tall = wide.shape[2]
    half = owned * KZ
    span = tall * KZ
    swaps = []
    for r in range(owned // tall):
        correlate(wide, sums, r, time_ways * frames, tall, atoms)
        at = half - (r + 1) * span
        arrange(sums, folded, mirror_fold, mirror, at, tall, True)
        swap = remote(
            mirror.at[:, :, pl.ds(at, span)], out_ref.at[:, :, pl.ds(at, span)],
            mirror_send.at[r], mirror_recv.at[r], opposite,
        )
        swap.start()
        swaps.append(swap)
        arrange(sums, folded, own_fold, out_ref, half + r * span, tall, False)

    for step in range(1, time_ways):
        mode_copy(step, 0, frames).wait_send()
    for step in range(1, chips):
        shipped(step).wait_send()
    for p in range(chips):
        relayed(p).wait_send()
    for swap in swaps:
        swap.wait()


def call(data, atom_ways, time_ways, rows, y_waves):
    frames, lanes = data.shape[1], data.shape[2]
    atoms = lanes * atom_ways
    group = KX // atom_ways
    blocks = atom_ways * lanes // LANES
    tall = min(8, rows)
    dims = (atom_ways, time_ways, y_waves, atoms)
    whole = pl.BlockSpec(memory_space=pltpu.VMEM)
    dma = pltpu.SemaphoreType.DMA
    tabled = pltpu.VMEM((blocks, KY // 2 * frames, LANES), jnp.float32)
    return pl.pallas_call(
        functools.partial(kernel, dims),
        out_shape=jax.ShapeDtypeStruct((COMPS, LAGS, 2 * rows * KZ), jnp.float32),
        in_specs=[whole],
        out_specs=whole,
        scratch_shapes=[
            pltpu.VMEM((atom_ways,) + data.shape, jnp.float32),
            pltpu.VMEM((blocks, 2 * (group - (group - 1) // 2), frames, LANES), jnp.float32),
            tabled, tabled, tabled, tabled,
            pltpu.VMEM((frames, LANES, group * KY), jnp.float32),
            pltpu.VMEM((time_ways, frames, rows, 2 * LANES), WIRE),
            pltpu.VMEM((time_ways, frames, rows, 2 * LANES), WIRE),
            pltpu.VMEM((2 * (rows // tall), time_ways * frames + LAGS, tall, LANES), jnp.float32),
            pltpu.VMEM((2, LAGS * tall, LANES), jnp.float32),
            pltpu.VMEM((LAGS * tall, LANES), jnp.float32),
            pltpu.VMEM((COMPS, LAGS, rows * KZ), jnp.float32),
            dma((atom_ways,)),
            dma((atom_ways // 2,)),
            dma((atom_ways // 2,)),
            dma((time_ways,)),
            dma((time_ways,)),
            dma((rows // tall,)),
            dma((rows // tall,)),
        ],
        compiler_params=pltpu.CompilerParams(
            vmem_limit_bytes=VMEM, collective_id=0, has_side_effects=True
        ),
        name="factors",
    )(data)


def per_device(positions, velocity):
    atom_ways = lax.axis_size("atom")
    time_ways = lax.axis_size("tm")
    owned = KX * KY // (atom_ways * time_ways)
    rows = owned // 2
    y_waves = [wave(q, KY) for q in range(KY) if q % owned >= rows]
    data = jnp.concatenate([positions.astype(jnp.float32), velocity.astype(jnp.float32)], 1)
    return call(jnp.transpose(data, (1, 0, 2)), atom_ways, time_ways, rows, y_waves)


def solution(mesh):
    in_specs = (P("tm", None, "atom"), P("tm", None, "atom"))
    out_specs = P(None, None, ("atom", "tm"))
    return jax.shard_map(
        per_device, mesh=mesh, in_specs=in_specs, out_specs=out_specs, check_vma=False
    )
```

```python
import functools
import math

import jax
import jax.numpy as jnp
from jax import lax
from jax.experimental import pallas as pl
from jax.experimental.pallas import tpu as pltpu
from jax.sharding import PartitionSpec as P

KX = 32
KY = 32
KZ = 32
LAGS = 16
LATTICE = 131072
QUARTER = LATTICE // 4
HALF_Z = KZ // 2
COMPS = 4
LANES = 128
VMEM = 56 * 1024 * 1024
WIRE = jnp.bfloat16


def wave(q, extent):
    return q - extent // 2 + (1 if q >= extent // 2 else 0)


def sincos(n):
    n = jnp.bitwise_and(n, LATTICE - 1)
    quadrant = jnp.right_shift(n + QUARTER // 2, 15)
    x = (n - jnp.left_shift(quadrant, 15)).astype(jnp.float32) * (2.0 * math.pi / LATTICE)
    y = x * x
    s = y * (1.0 / 362880.0) - 1.0 / 5040.0
    s = s * y + 1.0 / 120.0
    s = s * y - 1.0 / 6.0
    s = s * y * x + x
    c = y * (1.0 / 40320.0) - 1.0 / 720.0
    c = c * y + 1.0 / 24.0
    c = c * y - 0.5
    c = c * y + 1.0
    odd = jnp.bitwise_and(quadrant, 1) == 1
    cos = jnp.where(odd, s, c)
    sin = jnp.where(odd, c, s)
    cos = jnp.where(jnp.bitwise_and(quadrant + 1, 2) == 2, -cos, cos)
    sin = jnp.where(jnp.bitwise_and(quadrant, 2) == 2, -sin, sin)
    return cos, sin


def times(a, b):
    return a[0] * b[0] - a[1] * b[1], a[0] * b[1] + a[1] * b[0]


def plus_minus(a, b):
    cc, ss, cs, sc = a[0] * b[0], a[1] * b[1], a[0] * b[1], a[1] * b[0]
    return (cc - ss, sc + cs), (cc + ss, sc - cs)


def powers(e1):
    e = {1: e1}
    e[2] = times(e1, e1)
    e[3] = times(e[2], e1)
    e[4] = times(e[2], e[2])
    e[8] = times(e[4], e[4])
    e[12], _ = plus_minus(e[8], e[4])
    for d in (1, 2, 3):
        e[8 + d], e[8 - d] = plus_minus(e[8], e[d])
    e[16] = times(e[8], e[8])
    for d in (1, 2, 3):
        _, e[16 - d] = plus_minus(e[16], e[d])
    return e


def prepare(data, slot, first_block, xs, yc, ys, zc, zs, first_w, group, y_waves):
    middle = (group - 1) // 2
    frames = data.shape[2]

    def block(i):
        at = pl.ds(pl.multiple_of(i * LANES, LANES), LANES)
        to = first_block + i
        n = data[slot, 0, :, at].astype(jnp.int32)
        xs[to, 0], xs[to, 1] = sincos((first_w + middle) * n)
        e1 = sincos(n)
        e = {1: e1}
        for d in range(2, group - middle):
            e[d] = times(e[d - 1], e1)
        for d in range(1, group - middle):
            xs[to, 2 * d], xs[to, 2 * d + 1] = e[d]
        for c in range(COMPS - 1):
            xs[to, 2 * (group - middle) + c] = data[slot, 3 + c, :, at]
        e = powers(sincos(data[slot, 1, :, at].astype(jnp.int32)))
        for row, w in enumerate(y_waves):
            c, s = e[abs(w)]
            yc[to, row * frames : (row + 1) * frames, :] = c
            ys[to, row * frames : (row + 1) * frames, :] = s if w > 0 else -s
        e = powers(sincos(data[slot, 2, :, at].astype(jnp.int32)))
        for w in range(1, HALF_Z + 1):
            c, s = e[w]
            zc[to, (w - 1) * frames : w * frames, :] = c
            zs[to, (w - 1) * frames : w * frames, :] = s

    def step(i, _):
        block(2 * i)
        block(2 * i + 1)
        return 0

    lax.fori_loop(0, data.shape[3] // (2 * LANES), step, 0)


def frame_product(f, data, p, xs, yc, ys, zc, zs, lefts, rights, group, rows):
    middle = (group - 1) // 2
    lanes = data.shape[3]
    block = lefts.shape[2]
    steps = block // LANES

    def make(i):
        left, right = lefts.at[i % 2], rights.at[i % 2]
        for k in range(steps):
            n = p * (2 * lanes // LANES) + i * steps + k
            at = slice(k * LANES, (k + 1) * LANES)

            def put(j, e):
                for part in range(2):
                    row = (2 * j + part) * rows
                    left[row : row + rows, at] = e[part].astype(left.dtype)

            y = (yc[n, pl.ds(f, rows, stride=data.shape[2]), :], ys[n, pl.ds(f, rows, stride=data.shape[2]), :])
            mid = times((xs[n, 0, pl.ds(f, 1), :], xs[n, 1, pl.ds(f, 1), :]), y)
            put(middle, mid)
            for d in range(1, group - middle):
                up, down = plus_minus(mid, (xs[n, 2 * d, pl.ds(f, 1), :], xs[n, 2 * d + 1, pl.ds(f, 1), :]))
                put(middle + d, up)
                if middle - d >= 0:
                    put(middle - d, down)
            u = [xs[n, 2 * (group - middle) + c, pl.ds(f, 1), :] for c in range(COMPS - 1)]
            for part, ref in enumerate((zc, zs)):
                z = ref[n, pl.ds(f, HALF_Z, stride=data.shape[2]), :]
                for c in range(COMPS):
                    row = (part * COMPS + c) * HALF_Z
                    value = z if c == 0 else z * u[c - 1]
                    right[row : row + HALF_Z, at] = value.astype(right.dtype)

    number = 2 * lanes // block
    make(0)
    total = None
    for i in range(number):
        if i + 1 < number:
            make(i + 1)
        part = lax.dot_general(
            rights[i % 2], lefts[i % 2], (((1,), (1,)), ((), ())), preferred_element_type=jnp.float32
        )
        total = part if total is None else total + part
    return total


def combine(raw, group, rows):
    lane = lax.broadcasted_iota(jnp.int32, (rows, LANES), 1)
    sign = jnp.where(lane < LANES // 2, -1.0, 1.0)
    out = []
    for j in range(group):
        re = raw[2 * j * rows : (2 * j + 1) * rows]
        im = raw[(2 * j + 1) * rows : (2 * j + 2) * rows]
        turned = pltpu.roll(im, LANES // 2, 1) * sign
        out.append(jnp.concatenate([re + turned, re - turned], 1))
    return out


def fold_matrices():
    lane = lax.broadcasted_iota(jnp.int32, (LANES, LANES), 0)
    goal = lax.broadcasted_iota(jnp.int32, (LANES, LANES), 1)
    comp = jnp.right_shift(jnp.bitwise_and(lane, 63), 4)
    step = jnp.bitwise_and(lane, HALF_Z - 1)
    own = []
    for qz in (KZ // 2 + step, KZ // 2 - 1 - step):
        own.append(comp * KZ + qz)
    mirror = [comp * KZ + KZ - 1 - (t - comp * KZ) for t in own]
    return [[(goal == t).astype(jnp.float32).astype(jnp.bfloat16) for t in side] for side in (own, mirror)]


def exact_dot(x, matrix):
    high = x.astype(jnp.bfloat16)
    low = (x - high.astype(jnp.float32)).astype(jnp.bfloat16)
    return jnp.dot(high, matrix, preferred_element_type=jnp.float32) + jnp.dot(
        low, matrix, preferred_element_type=jnp.float32
    )


def widen(series, source, wide):
    frames, rows = series.shape[1], series.shape[2]
    tall = min(8, rows)
    for f in range(frames):
        block = series[source, f].astype(jnp.float32)
        for slot in range(wide.shape[0]):
            r, half = divmod(slot, 2)
            wide[slot, source * frames + f] = block[
                r * tall : (r + 1) * tall, half * LANES : (half + 1) * LANES
            ]


def correlate(wide, sums, r, frames, tall, atoms):
    anchors = 8
    for half in range(2):
        slot = 2 * r + half

        def step(i, acc):
            first = i * anchors
            window = [wide[slot, first + t] for t in range(LAGS)]
            for t in range(anchors):
                acc = tuple(acc[lag] + window[0] * window[lag] for lag in range(LAGS))
                window = window[1:]
                if t < anchors - 1:
                    window.append(wide[slot, first + t + LAGS])
            return acc

        zero = jnp.zeros((tall, LANES), jnp.float32)
        acc = lax.fori_loop(0, frames // anchors, step, (zero,) * LAGS)
        for lag in range(LAGS):
            sums[half, lag * tall : (lag + 1) * tall, :] = acc[lag] * (1.0 / (atoms * (frames - lag)))


def arrange(sums, folded, fold, out_ref, first_lane, rows, flip):
    groups = max(1, rows // 4)
    per = rows // groups
    lane = lax.broadcasted_iota(jnp.int32, (LAGS, LANES), 1)
    block = jnp.right_shift(lane, 5)
    folded[...] = exact_dot(sums[0], fold[0]) + exact_dot(sums[1], fold[1])
    for g in range(groups):
        parts = [folded[pl.ds(g * per + i, LAGS, stride=rows), :] for i in range(per)]
        if flip:
            parts = parts[::-1]
        goal = first_lane + (groups - 1 - g if flip else g) * LANES
        for c in range(COMPS):
            out = jnp.zeros((LAGS, LANES), jnp.float32)
            for i in range(per):
                shift = ((i - c) * KZ) % LANES
                part = parts[i] if shift == 0 else pltpu.roll(parts[i], shift, 1)
                out = jnp.where(block == i, part, out)
            out_ref[c, :, goal : goal + LANES] = out


def kernel(
    dims, data_ref, out_ref, data, xs, yc, ys, zc, zs, lefts, rights, total, stage, series, wide, sums, folded,
    mirror, in_recv, x_send, relay_send, mode_send, mode_recv, mirror_send, mirror_recv,
):
    atom_ways, time_ways, y_waves, atoms = dims
    frames = data.shape[2]
    group = KX // atom_ways
    rows = KY // 2
    owned = stage.shape[2]
    split = rows // owned
    chips = atom_ways // 2
    a, t = lax.axis_index("atom"), lax.axis_index("tm")
    chip, core = a // 2, a % 2
    first = a * group
    first_w = first - KX // 2 + (first >= KX // 2).astype(jnp.int32)

    mate = (chip * 2 + 1 - core, t)
    opposite = (atom_ways - 1 - a, time_ways - 1 - t)

    def along_x(step):
        return (((chip + step) % chips) * 2 + core, t)

    def along_time(step):
        return (t + step) % time_ways

    def signal(device):
        pl.semaphore_signal(
            pltpu.get_barrier_semaphore(), inc=1, device_id=device, device_id_type=pl.DeviceIdType.MESH
        )

    def remote(src, dst, send, recv, device):
        return pltpu.make_async_remote_copy(
            src_ref=src, dst_ref=dst, send_sem=send, recv_sem=recv, device_id=device,
            device_id_type=pl.DeviceIdType.MESH,
        )

    signal(mate)
    signal(opposite)
    for step in range(1, chips):
        signal(along_x(step))
    for step in range(1, time_ways):
        signal((a, along_time(step)))

    data[0] = data_ref[...]
    for slot in range(wide.shape[0]):
        for lag in range(LAGS):
            wide[slot, time_ways * frames + lag] = jnp.zeros(wide.shape[2:], jnp.float32)
    pl.semaphore_wait(pltpu.get_barrier_semaphore(), chips + time_ways)

    def shipped(step):
        return remote(data.at[0], data.at[2 * step], x_send.at[step], in_recv.at[2 * step], along_x(step))

    def relayed(p):
        return remote(
            data.at[2 * p], data.at[2 * p + 1], relay_send.at[p], in_recv.at[2 * p + 1], mate
        )

    def mode_copy(step, f, count):
        goal, at = along_time(step), pl.ds(f, count)
        return remote(
            stage.at[goal, at], series.at[t, at], mode_send.at[step], mode_recv.at[step], (a, goal)
        )

    def mode_arrival(step):
        source = (t + time_ways - step) % time_ways
        return remote(
            stage.at[source], series.at[source], mode_send.at[step], mode_recv.at[step], (a, source)
        )

    for step in range(1, chips):
        shipped(step).start()

    blocks = data.shape[3] // LANES

    def tables(p):
        if p > 0:
            shipped(p).wait_recv()
        relayed(p).start()
        prepare(data, 2 * p, 2 * p * blocks, xs, yc, ys, zc, zs, first_w, group, y_waves)
        relayed(p).wait_recv()
        prepare(data, 2 * p + 1, (2 * p + 1) * blocks, xs, yc, ys, zc, zs, first_w, group, y_waves)

    def product(f, p):
        return frame_product(f, data, p, xs, yc, ys, zc, zs, lefts, rights, group, rows)

    def emit(f):
        for j, block in enumerate(combine(jnp.transpose(total[f]), group, rows)):
            block = block.astype(stage.dtype)
            for k in range(split):
                stage[j * split + k, f] = block[k * owned : (k + 1) * owned]
        series[t, f] = stage[t, f]
        for step in range(1, time_ways):
            mode_copy(step, f, 1).start()

    early = frames * 5 // 8

    def own_part(f, _):
        total[f] = product(f, 0)
        return 0

    tables(0)
    lax.fori_loop(0, early, own_part, 0)
    for p in range(1, chips):
        tables(p)

        def far_part(f, _):
            total[f] += product(f, p)
            if p == chips - 1:
                emit(f)
            return 0

        lax.fori_loop(0, early, far_part, 0)

    def whole_frame(f, _):
        total[f] = jnp.zeros(total.shape[1:], jnp.float32)

        def part(p, _):
            total[f] += product(f, p)
            return 0

        lax.fori_loop(0, chips, part, 0)
        emit(f)
        return 0

    lax.fori_loop(early, frames, whole_frame, 0)

    widen(series, t, wide)
    for step in range(1, time_ways):
        mode_arrival(step).wait_recv()
        widen(series, (t + time_ways - step) % time_ways, wide)

    own_fold, mirror_fold = fold_matrices()
    tall = wide.shape[2]
    half = owned * KZ
    span = tall * KZ
    swaps = []
    for r in range(owned // tall):
        correlate(wide, sums, r, time_ways * frames, tall, atoms)
        at = half - (r + 1) * span
        arrange(sums, folded, mirror_fold, mirror, at, tall, True)
        swap = remote(
            mirror.at[:, :, pl.ds(at, span)], out_ref.at[:, :, pl.ds(at, span)],
            mirror_send.at[r], mirror_recv.at[r], opposite,
        )
        swap.start()
        swaps.append(swap)
        arrange(sums, folded, own_fold, out_ref, half + r * span, tall, False)

    for step in range(1, time_ways):
        mode_copy(step, 0, frames).wait_send()
    for step in range(1, chips):
        shipped(step).wait_send()
    for p in range(chips):
        relayed(p).wait_send()
    for swap in swaps:
        swap.wait()


def call(data, atom_ways, time_ways, rows, y_waves):
    frames, lanes = data.shape[1], data.shape[2]
    atoms = lanes * atom_ways
    group = KX // atom_ways
    blocks = atom_ways * lanes // LANES
    tall = min(8, rows)
    dims = (atom_ways, time_ways, y_waves, atoms)
    whole = pl.BlockSpec(memory_space=pltpu.VMEM)
    dma = pltpu.SemaphoreType.DMA
    tabled = pltpu.VMEM((blocks, KY // 2 * frames, LANES), jnp.float32)
    return pl.pallas_call(
        functools.partial(kernel, dims),
        out_shape=jax.ShapeDtypeStruct((COMPS, LAGS, 2 * rows * KZ), jnp.float32),
        in_specs=[whole],
        out_specs=whole,
        scratch_shapes=[
            pltpu.VMEM((atom_ways,) + data.shape, jnp.float32),
            pltpu.VMEM((blocks, 2 * (group - (group - 1) // 2) + COMPS - 1, frames, LANES), jnp.float32),
            tabled, tabled, tabled, tabled,
            pltpu.VMEM((2, group * KY, math.gcd(lanes, 1024)), jnp.bfloat16),
            pltpu.VMEM((2, LANES, math.gcd(lanes, 1024)), jnp.bfloat16),
            pltpu.VMEM((frames, LANES, group * KY), jnp.float32),
            pltpu.VMEM((time_ways, frames, rows, 2 * LANES), WIRE),
            pltpu.VMEM((time_ways, frames, rows, 2 * LANES), WIRE),
            pltpu.VMEM((2 * (rows // tall), time_ways * frames + LAGS, tall, LANES), jnp.float32),
            pltpu.VMEM((2, LAGS * tall, LANES), jnp.float32),
            pltpu.VMEM((LAGS * tall, LANES), jnp.float32),
            pltpu.VMEM((COMPS, LAGS, rows * KZ), jnp.float32),
            dma((atom_ways,)),
            dma((atom_ways // 2,)),
            dma((atom_ways // 2,)),
            dma((time_ways,)),
            dma((time_ways,)),
            dma((rows // tall,)),
            dma((rows // tall,)),
        ],
        compiler_params=pltpu.CompilerParams(
            vmem_limit_bytes=VMEM, collective_id=0, has_side_effects=True
        ),
        name="factors",
    )(data)


def per_device(positions, velocity):
    atom_ways = lax.axis_size("atom")
    time_ways = lax.axis_size("tm")
    owned = KX * KY // (atom_ways * time_ways)
    rows = owned // 2
    y_waves = [wave(q, KY) for q in range(KY) if q % owned >= rows]
    data = jnp.concatenate([positions.astype(jnp.float32), velocity.astype(jnp.float32)], 1)
    return call(jnp.transpose(data, (1, 0, 2)), atom_ways, time_ways, rows, y_waves)


def solution(mesh):
    in_specs = (P("tm", None, "atom"), P("tm", None, "atom"))
    out_specs = P(None, None, ("atom", "tm"))
    return jax.shard_map(
        per_device, mesh=mesh, in_specs=in_specs, out_specs=out_specs, check_vma=False
    )
```

```python
import functools
import math

import jax
import jax.numpy as jnp
from jax import lax
from jax.experimental import pallas as pl
from jax.experimental.pallas import tpu as pltpu
from jax.sharding import PartitionSpec as P

KX = 32
KY = 32
KZ = 32
LAGS = 16
LATTICE = 131072
QUARTER = LATTICE // 4
HALF_Z = KZ // 2
COMPS = 4
LANES = 128
VMEM = 56 * 1024 * 1024
WIRE = jnp.bfloat16


def wave(q, extent):
    return q - extent // 2 + (1 if q >= extent // 2 else 0)


def sincos(n):
    n = jnp.bitwise_and(n, LATTICE - 1)
    quadrant = jnp.right_shift(n + QUARTER // 2, 15)
    x = (n - jnp.left_shift(quadrant, 15)).astype(jnp.float32) * (2.0 * math.pi / LATTICE)
    y = x * x
    s = y * (1.0 / 362880.0) - 1.0 / 5040.0
    s = s * y + 1.0 / 120.0
    s = s * y - 1.0 / 6.0
    s = s * y * x + x
    c = y * (1.0 / 40320.0) - 1.0 / 720.0
    c = c * y + 1.0 / 24.0
    c = c * y - 0.5
    c = c * y + 1.0
    odd = jnp.bitwise_and(quadrant, 1) == 1
    cos = jnp.where(odd, s, c)
    sin = jnp.where(odd, c, s)
    cos = jnp.where(jnp.bitwise_and(quadrant + 1, 2) == 2, -cos, cos)
    sin = jnp.where(jnp.bitwise_and(quadrant, 2) == 2, -sin, sin)
    return cos, sin


def times(a, b):
    return a[0] * b[0] - a[1] * b[1], a[0] * b[1] + a[1] * b[0]


def plus_minus(a, b):
    cc, ss, cs, sc = a[0] * b[0], a[1] * b[1], a[0] * b[1], a[1] * b[0]
    return (cc - ss, sc + cs), (cc + ss, sc - cs)


def powers(e1):
    e = {1: e1}
    e[2] = times(e1, e1)
    e[3] = times(e[2], e1)
    e[4] = times(e[2], e[2])
    e[8] = times(e[4], e[4])
    e[12], _ = plus_minus(e[8], e[4])
    for d in (1, 2, 3):
        e[8 + d], e[8 - d] = plus_minus(e[8], e[d])
    e[16] = times(e[8], e[8])
    for d in (1, 2, 3):
        _, e[16 - d] = plus_minus(e[16], e[d])
    return e


def prepare(data, slot, first_block, xs, yc, ys, zc, zs, first_w, group, y_waves):
    middle = (group - 1) // 2
    frames = data.shape[2]
    pitch = frames + 1

    def block(i):
        at = pl.ds(pl.multiple_of(i * LANES, LANES), LANES)
        to = first_block + i
        n = data[slot, 0, :, at].astype(jnp.int32)
        xs[to, 0], xs[to, 1] = sincos((first_w + middle) * n)
        e1 = sincos(n)
        e = {1: e1}
        for d in range(2, group - middle):
            e[d] = times(e[d - 1], e1)
        for d in range(1, group - middle):
            xs[to, 2 * d], xs[to, 2 * d + 1] = e[d]
        for c in range(COMPS - 1):
            xs[to, 2 * (group - middle) + c] = data[slot, 3 + c, :, at]
        e = powers(sincos(data[slot, 1, :, at].astype(jnp.int32)))
        for row, w in enumerate(y_waves):
            c, s = e[abs(w)]
            yc[to, row * pitch : row * pitch + frames, :] = c
            ys[to, row * pitch : row * pitch + frames, :] = s if w > 0 else -s
        e = powers(sincos(data[slot, 2, :, at].astype(jnp.int32)))
        for w in range(1, HALF_Z + 1):
            c, s = e[w]
            zc[to, (w - 1) * pitch : (w - 1) * pitch + frames, :] = c
            zs[to, (w - 1) * pitch : (w - 1) * pitch + frames, :] = s

    def step(i, _):
        block(2 * i)
        block(2 * i + 1)
        return 0

    lax.fori_loop(0, data.shape[3] // (2 * LANES), step, 0)


def frame_product(f, data, p, xs, yc, ys, zc, zs, block, group, rows):
    middle = (group - 1) // 2
    frames, lanes = data.shape[2], data.shape[3]
    steps = block // LANES

    def make(n):
        left = [None] * (2 * group)

        def put(j, e):
            left[2 * j], left[2 * j + 1] = e[0].astype(jnp.bfloat16), e[1].astype(jnp.bfloat16)

        def row(j):
            return xs[n, j, pl.ds(f, 1), :]

        def pick(ref):
            return ref[n, pl.ds(f, rows, stride=frames + 1), :]

        mid = times((row(0), row(1)), (pick(yc), pick(ys)))
        put(middle, mid)
        for d in range(1, group - middle):
            up, down = plus_minus(mid, (row(2 * d), row(2 * d + 1)))
            put(middle + d, up)
            if middle - d >= 0:
                put(middle - d, down)
        right = []
        u = [row(2 * (group - middle) + c) for c in range(COMPS - 1)]
        for ref in (zc, zs):
            z = pick(ref)
            right.append(z.astype(jnp.bfloat16))
            right += [(z * weight).astype(jnp.bfloat16) for weight in u]
        return jnp.concatenate(left, 0), jnp.concatenate(right, 0)

    total = None
    for i in range(2 * lanes // block):
        first = p * (2 * lanes // LANES) + i * steps
        made = [make(first + k) for k in range(steps)]
        left, right = (jnp.concatenate(list(side), 1) for side in zip(*made))
        part = lax.dot_general(
            left, right, (((1,), (1,)), ((), ())), preferred_element_type=jnp.float32
        )
        total = part if total is None else total + part
    return total


def combine(raw, group, rows):
    lane = lax.broadcasted_iota(jnp.int32, (rows, LANES), 1)
    sign = jnp.where(lane < LANES // 2, -1.0, 1.0)
    out = []
    for j in range(group):
        re = raw[2 * j * rows : (2 * j + 1) * rows]
        im = raw[(2 * j + 1) * rows : (2 * j + 2) * rows]
        turned = pltpu.roll(im, LANES // 2, 1) * sign
        out.append(jnp.concatenate([re + turned, re - turned], 1))
    return out


def fold_matrices():
    lane = lax.broadcasted_iota(jnp.int32, (LANES, LANES), 0)
    goal = lax.broadcasted_iota(jnp.int32, (LANES, LANES), 1)
    comp = jnp.right_shift(jnp.bitwise_and(lane, 63), 4)
    step = jnp.bitwise_and(lane, HALF_Z - 1)
    own = []
    for qz in (KZ // 2 + step, KZ // 2 - 1 - step):
        own.append(comp * KZ + qz)
    mirror = [comp * KZ + KZ - 1 - (t - comp * KZ) for t in own]
    return [[(goal == t).astype(jnp.float32).astype(jnp.bfloat16) for t in side] for side in (own, mirror)]


def exact_dot(x, matrix):
    high = x.astype(jnp.bfloat16)
    low = (x - high.astype(jnp.float32)).astype(jnp.bfloat16)
    return jnp.dot(high, matrix, preferred_element_type=jnp.float32) + jnp.dot(
        low, matrix, preferred_element_type=jnp.float32
    )


def widen(series, source, wide):
    frames, rows = series.shape[1], series.shape[2]
    tall = min(8, rows)
    for f in range(frames):
        block = series[source, f].astype(jnp.float32)
        for slot in range(wide.shape[0]):
            r, half = divmod(slot, 2)
            wide[slot, source * frames + f] = block[
                r * tall : (r + 1) * tall, half * LANES : (half + 1) * LANES
            ]


def correlate(wide, sums, r, frames, tall, atoms):
    anchors = 8
    for half in range(2):
        slot = 2 * r + half

        def step(i, acc):
            first = i * anchors
            window = [wide[slot, first + t] for t in range(LAGS)]
            for t in range(anchors):
                acc = tuple(acc[lag] + window[0] * window[lag] for lag in range(LAGS))
                window = window[1:]
                if t < anchors - 1:
                    window.append(wide[slot, first + t + LAGS])
            return acc

        zero = jnp.zeros((tall, LANES), jnp.float32)
        acc = lax.fori_loop(0, frames // anchors, step, (zero,) * LAGS)
        for lag in range(LAGS):
            sums[half, lag * tall : (lag + 1) * tall, :] = acc[lag] * (1.0 / (atoms * (frames - lag)))


def arrange(sums, folded, fold, out_ref, first_lane, rows, flip):
    groups = max(1, rows // 4)
    per = rows // groups
    lane = lax.broadcasted_iota(jnp.int32, (LAGS, LANES), 1)
    block = jnp.right_shift(lane, 5)
    folded[...] = exact_dot(sums[0], fold[0]) + exact_dot(sums[1], fold[1])
    for g in range(groups):
        parts = [folded[pl.ds(g * per + i, LAGS, stride=rows), :] for i in range(per)]
        if flip:
            parts = parts[::-1]
        goal = first_lane + (groups - 1 - g if flip else g) * LANES
        for c in range(COMPS):
            out = jnp.zeros((LAGS, LANES), jnp.float32)
            for i in range(per):
                shift = ((i - c) * KZ) % LANES
                part = parts[i] if shift == 0 else pltpu.roll(parts[i], shift, 1)
                out = jnp.where(block == i, part, out)
            out_ref[c, :, goal : goal + LANES] = out


def kernel(
    dims, data_ref, out_ref, data, xs, yc, ys, zc, zs, total, stage, series, wide, sums, folded,
    mirror, in_recv, x_send, relay_send, mode_send, mode_recv, mirror_send, mirror_recv,
):
    atom_ways, time_ways, y_waves, atoms = dims
    frames = data.shape[2]
    group = KX // atom_ways
    rows = KY // 2
    owned = stage.shape[2]
    split = rows // owned
    chips = atom_ways // 2
    a, t = lax.axis_index("atom"), lax.axis_index("tm")
    chip, core = a // 2, a % 2
    first = a * group
    first_w = first - KX // 2 + (first >= KX // 2).astype(jnp.int32)

    mate = (chip * 2 + 1 - core, t)
    opposite = (atom_ways - 1 - a, time_ways - 1 - t)

    def along_x(step):
        return (((chip + step) % chips) * 2 + core, t)

    def along_time(step):
        return (t + step) % time_ways

    def signal(device):
        pl.semaphore_signal(
            pltpu.get_barrier_semaphore(), inc=1, device_id=device, device_id_type=pl.DeviceIdType.MESH
        )

    def remote(src, dst, send, recv, device):
        return pltpu.make_async_remote_copy(
            src_ref=src, dst_ref=dst, send_sem=send, recv_sem=recv, device_id=device,
            device_id_type=pl.DeviceIdType.MESH,
        )

    signal(mate)
    signal(opposite)
    for step in range(1, chips):
        signal(along_x(step))
    for step in range(1, time_ways):
        signal((a, along_time(step)))

    data[0] = data_ref[...]
    for slot in range(wide.shape[0]):
        for lag in range(LAGS):
            wide[slot, time_ways * frames + lag] = jnp.zeros(wide.shape[2:], jnp.float32)
    pl.semaphore_wait(pltpu.get_barrier_semaphore(), chips + time_ways)

    def shipped(step):
        return remote(data.at[0], data.at[2 * step], x_send.at[step], in_recv.at[2 * step], along_x(step))

    def relayed(p):
        return remote(
            data.at[2 * p], data.at[2 * p + 1], relay_send.at[p], in_recv.at[2 * p + 1], mate
        )

    def mode_copy(step, f, count):
        goal, at = along_time(step), pl.ds(f, count)
        return remote(
            stage.at[goal, at], series.at[t, at], mode_send.at[step], mode_recv.at[step], (a, goal)
        )

    def mode_arrival(step):
        source = (t + time_ways - step) % time_ways
        return remote(
            stage.at[source], series.at[source], mode_send.at[step], mode_recv.at[step], (a, source)
        )

    for step in range(1, chips):
        shipped(step).start()

    blocks = data.shape[3] // LANES

    def tables(p):
        if p > 0:
            shipped(p).wait_recv()
        relayed(p).start()
        prepare(data, 2 * p, 2 * p * blocks, xs, yc, ys, zc, zs, first_w, group, y_waves)
        relayed(p).wait_recv()
        prepare(data, 2 * p + 1, (2 * p + 1) * blocks, xs, yc, ys, zc, zs, first_w, group, y_waves)

    def product(f, p):
        return frame_product(f, data, p, xs, yc, ys, zc, zs, 4 * LANES, group, rows)

    def emit(f):
        for j, block in enumerate(combine(total[f], group, rows)):
            block = block.astype(stage.dtype)
            for k in range(split):
                stage[j * split + k, f] = block[k * owned : (k + 1) * owned]
        series[t, f] = stage[t, f]
        for step in range(1, time_ways):
            mode_copy(step, f, 1).start()

    early = frames * 5 // 8

    def own_part(f, _):
        total[f] = product(f, 0)
        return 0

    tables(0)
    lax.fori_loop(0, early, own_part, 0)
    for p in range(1, chips):
        tables(p)

        def far_part(f, _):
            total[f] += product(f, p)
            if p == chips - 1:
                emit(f)
            return 0

        lax.fori_loop(0, early, far_part, 0)

    def whole_frame(f, _):
        total[f] = jnp.zeros(total.shape[1:], jnp.float32)

        def part(p, _):
            total[f] += product(f, p)
            return 0

        lax.fori_loop(0, chips, part, 0)
        emit(f)
        return 0

    lax.fori_loop(early, frames, whole_frame, 0)

    widen(series, t, wide)
    for step in range(1, time_ways):
        mode_arrival(step).wait_recv()
        widen(series, (t + time_ways - step) % time_ways, wide)

    own_fold, mirror_fold = fold_matrices()
    tall = wide.shape[2]
    half = owned * KZ
    span = tall * KZ
    swaps = []
    for r in range(owned // tall):
        correlate(wide, sums, r, time_ways * frames, tall, atoms)
        at = half - (r + 1) * span
        arrange(sums, folded, mirror_fold, mirror, at, tall, True)
        swap = remote(
            mirror.at[:, :, pl.ds(at, span)], out_ref.at[:, :, pl.ds(at, span)],
            mirror_send.at[r], mirror_recv.at[r], opposite,
        )
        swap.start()
        swaps.append(swap)
        arrange(sums, folded, own_fold, out_ref, half + r * span, tall, False)

    for step in range(1, time_ways):
        mode_copy(step, 0, frames).wait_send()
    for step in range(1, chips):
        shipped(step).wait_send()
    for p in range(chips):
        relayed(p).wait_send()
    for swap in swaps:
        swap.wait()


def call(data, atom_ways, time_ways, rows, y_waves):
    frames, lanes = data.shape[1], data.shape[2]
    atoms = lanes * atom_ways
    group = KX // atom_ways
    blocks = atom_ways * lanes // LANES
    tall = min(8, rows)
    dims = (atom_ways, time_ways, y_waves, atoms)
    whole = pl.BlockSpec(memory_space=pltpu.VMEM)
    dma = pltpu.SemaphoreType.DMA
    tabled = pltpu.VMEM((blocks, KY // 2 * (frames + 1), LANES), jnp.float32)
    return pl.pallas_call(
        functools.partial(kernel, dims),
        out_shape=jax.ShapeDtypeStruct((COMPS, LAGS, 2 * rows * KZ), jnp.float32),
        in_specs=[whole],
        out_specs=whole,
        scratch_shapes=[
            pltpu.VMEM((atom_ways,) + data.shape, jnp.float32),
            pltpu.VMEM((blocks, 2 * (group - (group - 1) // 2) + COMPS - 1, frames, LANES), jnp.float32),
            tabled, tabled, tabled, tabled,
            pltpu.VMEM((frames, group * KY, LANES), jnp.float32),
            pltpu.VMEM((time_ways, frames, rows, 2 * LANES), WIRE),
            pltpu.VMEM((time_ways, frames, rows, 2 * LANES), WIRE),
            pltpu.VMEM((2 * (rows // tall), time_ways * frames + LAGS, tall, LANES), jnp.float32),
            pltpu.VMEM((2, LAGS * tall, LANES), jnp.float32),
            pltpu.VMEM((LAGS * tall, LANES), jnp.float32),
            pltpu.VMEM((COMPS, LAGS, rows * KZ), jnp.float32),
            dma((atom_ways,)),
            dma((atom_ways // 2,)),
            dma((atom_ways // 2,)),
            dma((time_ways,)),
            dma((time_ways,)),
            dma((rows // tall,)),
            dma((rows // tall,)),
        ],
        compiler_params=pltpu.CompilerParams(
            vmem_limit_bytes=VMEM, collective_id=0, has_side_effects=True
        ),
        name="factors",
    )(data)


def per_device(positions, velocity):
    atom_ways = lax.axis_size("atom")
    time_ways = lax.axis_size("tm")
    owned = KX * KY // (atom_ways * time_ways)
    rows = owned // 2
    y_waves = [wave(q, KY) for q in range(KY) if q % owned >= rows]
    data = jnp.concatenate([positions.astype(jnp.float32), velocity.astype(jnp.float32)], 1)
    return call(jnp.transpose(data, (1, 0, 2)), atom_ways, time_ways, rows, y_waves)


def solution(mesh):
    in_specs = (P("tm", None, "atom"), P("tm", None, "atom"))
    out_specs = P(None, None, ("atom", "tm"))
    return jax.shard_map(
        per_device, mesh=mesh, in_specs=in_specs, out_specs=out_specs, check_vma=False
    )
```

```python
import functools
import math

import jax
import jax.numpy as jnp
from jax import lax
from jax.experimental import pallas as pl
from jax.experimental.pallas import tpu as pltpu
from jax.sharding import PartitionSpec as P

KX = 32
KY = 32
KZ = 32
LAGS = 16
LATTICE = 131072
QUARTER = LATTICE // 4
HALF_Z = KZ // 2
COMPS = 4
LANES = 128
VMEM = 56 * 1024 * 1024
WIRE = jnp.bfloat16


def wave(q, extent):
    return q - extent // 2 + (1 if q >= extent // 2 else 0)


def sincos(n):
    n = jnp.bitwise_and(n, LATTICE - 1)
    quadrant = jnp.right_shift(n + QUARTER // 2, 15)
    x = (n - jnp.left_shift(quadrant, 15)).astype(jnp.float32) * (2.0 * math.pi / LATTICE)
    y = x * x
    s = y * (1.0 / 362880.0) - 1.0 / 5040.0
    s = s * y + 1.0 / 120.0
    s = s * y - 1.0 / 6.0
    s = s * y * x + x
    c = y * (1.0 / 40320.0) - 1.0 / 720.0
    c = c * y + 1.0 / 24.0
    c = c * y - 0.5
    c = c * y + 1.0
    odd = jnp.bitwise_and(quadrant, 1) == 1
    cos = jnp.where(odd, s, c)
    sin = jnp.where(odd, c, s)
    cos = jnp.where(jnp.bitwise_and(quadrant + 1, 2) == 2, -cos, cos)
    sin = jnp.where(jnp.bitwise_and(quadrant, 2) == 2, -sin, sin)
    return cos, sin


def times(a, b):
    return a[0] * b[0] - a[1] * b[1], a[0] * b[1] + a[1] * b[0]


def plus_minus(a, b):
    cc, ss, cs, sc = a[0] * b[0], a[1] * b[1], a[0] * b[1], a[1] * b[0]
    return (cc - ss, sc + cs), (cc + ss, sc - cs)


def powers(e1):
    e = {1: e1}
    e[2] = times(e1, e1)
    e[3] = times(e[2], e1)
    e[4] = times(e[2], e[2])
    e[8] = times(e[4], e[4])
    e[12], _ = plus_minus(e[8], e[4])
    for d in (1, 2, 3):
        e[8 + d], e[8 - d] = plus_minus(e[8], e[d])
    e[16] = times(e[8], e[8])
    for d in (1, 2, 3):
        _, e[16 - d] = plus_minus(e[16], e[d])
    return e


def prepare(data, slot, first_block, xs, yc, ys, zc, zs, first_w, group, y_waves):
    middle = (group - 1) // 2
    frames = data.shape[2]
    pitch = frames + 1

    def block(i):
        at = pl.ds(pl.multiple_of(i * LANES, LANES), LANES)
        to = first_block + i
        n = data[slot, 0, :, at].astype(jnp.int32)
        xs[to, 0], xs[to, 1] = sincos((first_w + middle) * n)
        e1 = sincos(n)
        e = {1: e1}
        for d in range(2, group - middle):
            e[d] = times(e[d - 1], e1)
        for d in range(1, group - middle):
            xs[to, 2 * d], xs[to, 2 * d + 1] = e[d]
        for c in range(COMPS - 1):
            xs[to, 2 * (group - middle) + c] = data[slot, 3 + c, :, at]
        e = powers(sincos(data[slot, 1, :, at].astype(jnp.int32)))
        for row, w in enumerate(y_waves):
            c, s = e[abs(w)]
            yc[to, row * pitch : row * pitch + frames, :] = c
            ys[to, row * pitch : row * pitch + frames, :] = s if w > 0 else -s
        e = powers(sincos(data[slot, 2, :, at].astype(jnp.int32)))
        for w in range(1, HALF_Z + 1):
            c, s = e[w]
            zc[to, (w - 1) * pitch : (w - 1) * pitch + frames, :] = c
            zs[to, (w - 1) * pitch : (w - 1) * pitch + frames, :] = s

    def step(i, _):
        block(2 * i)
        block(2 * i + 1)
        return 0

    lax.fori_loop(0, data.shape[3] // (2 * LANES), step, 0)


def frame_product(f, data, p, xs, yc, ys, zc, zs, block, group, rows):
    middle = (group - 1) // 2
    frames, lanes = data.shape[2], data.shape[3]
    steps = block // LANES

    def make(n):
        left = [None] * (2 * group)

        def put(j, e):
            left[2 * j], left[2 * j + 1] = e[0].astype(jnp.bfloat16), e[1].astype(jnp.bfloat16)

        def row(j):
            return xs[n, j, pl.ds(f, 1), :]

        def pick(ref):
            return ref[n, pl.ds(f, rows, stride=frames + 1), :]

        mid = times((row(0), row(1)), (pick(yc), pick(ys)))
        put(middle, mid)
        for d in range(1, group - middle):
            up, down = plus_minus(mid, (row(2 * d), row(2 * d + 1)))
            put(middle + d, up)
            if middle - d >= 0:
                put(middle - d, down)
        right = []
        u = [row(2 * (group - middle) + c) for c in range(COMPS - 1)]
        for ref in (zc, zs):
            z = pick(ref)
            right.append(z.astype(jnp.bfloat16))
            right += [(z * weight).astype(jnp.bfloat16) for weight in u]
        return jnp.concatenate(left, 0), jnp.concatenate(right, 0)

    total = None
    for i in range(2 * lanes // block):
        first = p * (2 * lanes // LANES) + i * steps
        made = [make(first + k) for k in range(steps)]
        left, right = (jnp.concatenate(list(side), 1) for side in zip(*made))
        part = lax.dot_general(
            left, right, (((1,), (1,)), ((), ())), preferred_element_type=jnp.float32
        )
        total = part if total is None else total + part
    return total


def combine(raw, group, rows):
    lane = lax.broadcasted_iota(jnp.int32, (rows, LANES), 1)
    sign = jnp.where(lane < LANES // 2, -1.0, 1.0)
    out = []
    for j in range(group):
        re = raw[2 * j * rows : (2 * j + 1) * rows]
        im = raw[(2 * j + 1) * rows : (2 * j + 2) * rows]
        turned = pltpu.roll(im, LANES // 2, 1) * sign
        out.append(jnp.concatenate([re + turned, re - turned], 1))
    return out


def fold_matrices():
    lane = lax.broadcasted_iota(jnp.int32, (LANES, LANES), 0)
    goal = lax.broadcasted_iota(jnp.int32, (LANES, LANES), 1)
    comp = jnp.right_shift(jnp.bitwise_and(lane, 63), 4)
    step = jnp.bitwise_and(lane, HALF_Z - 1)
    own = []
    for qz in (KZ // 2 + step, KZ // 2 - 1 - step):
        own.append(comp * KZ + qz)
    mirror = [comp * KZ + KZ - 1 - (t - comp * KZ) for t in own]
    return [[(goal == t).astype(jnp.float32).astype(jnp.bfloat16) for t in side] for side in (own, mirror)]


def exact_dot(x, matrix):
    high = x.astype(jnp.bfloat16)
    low = (x - high.astype(jnp.float32)).astype(jnp.bfloat16)
    return jnp.dot(high, matrix, preferred_element_type=jnp.float32) + jnp.dot(
        low, matrix, preferred_element_type=jnp.float32
    )


def widen(series, source, wide):
    frames, rows = series.shape[1], series.shape[2]
    tall = min(8, rows)
    for f in range(frames):
        block = series[source, f].astype(jnp.float32)
        for slot in range(wide.shape[0]):
            r, half = divmod(slot, 2)
            wide[slot, source * frames + f] = block[
                r * tall : (r + 1) * tall, half * LANES : (half + 1) * LANES
            ]


def correlate(wide, sums, r, frames, tall, atoms):
    anchors = 8
    for half in range(2):
        slot = 2 * r + half

        def step(i, acc):
            first = i * anchors
            window = [wide[slot, first + t] for t in range(LAGS)]
            for t in range(anchors):
                acc = tuple(acc[lag] + window[0] * window[lag] for lag in range(LAGS))
                window = window[1:]
                if t < anchors - 1:
                    window.append(wide[slot, first + t + LAGS])
            return acc

        zero = jnp.zeros((tall, LANES), jnp.float32)
        acc = lax.fori_loop(0, frames // anchors, step, (zero,) * LAGS)
        for lag in range(LAGS):
            sums[half, lag * tall : (lag + 1) * tall, :] = acc[lag] * (1.0 / (atoms * (frames - lag)))


def arrange(sums, folded, fold, out_ref, first_lane, rows, flip):
    groups = max(1, rows // 4)
    per = rows // groups
    lane = lax.broadcasted_iota(jnp.int32, (LAGS, LANES), 1)
    block = jnp.right_shift(lane, 5)
    folded[...] = exact_dot(sums[0], fold[0]) + exact_dot(sums[1], fold[1])
    for g in range(groups):
        parts = [folded[pl.ds(g * per + i, LAGS, stride=rows), :] for i in range(per)]
        if flip:
            parts = parts[::-1]
        goal = first_lane + (groups - 1 - g if flip else g) * LANES
        for c in range(COMPS):
            out = jnp.zeros((LAGS, LANES), jnp.float32)
            for i in range(per):
                shift = ((i - c) * KZ) % LANES
                part = parts[i] if shift == 0 else pltpu.roll(parts[i], shift, 1)
                out = jnp.where(block == i, part, out)
            out_ref[c, :, goal : goal + LANES] = out


def kernel(
    dims, pos_ref, vel_ref, out_ref, data, xs, yc, ys, zc, zs, total, stage, series, wide, sums, folded,
    mirror, in_recv, x_send, relay_send, mode_send, mode_recv, mirror_send, mirror_recv,
):
    atom_ways, time_ways, y_waves, atoms = dims
    frames = data.shape[2]
    group = KX // atom_ways
    rows = KY // 2
    owned = stage.shape[2]
    split = rows // owned
    chips = atom_ways // 2
    a, t = lax.axis_index("atom"), lax.axis_index("tm")
    chip, core = a // 2, a % 2
    first = a * group
    first_w = first - KX // 2 + (first >= KX // 2).astype(jnp.int32)

    mate = (chip * 2 + 1 - core, t)
    opposite = (atom_ways - 1 - a, time_ways - 1 - t)

    def along_x(step):
        return (((chip + step) % chips) * 2 + core, t)

    def along_time(step):
        return (t + step) % time_ways

    def signal(device):
        pl.semaphore_signal(
            pltpu.get_barrier_semaphore(), inc=1, device_id=device, device_id_type=pl.DeviceIdType.MESH
        )

    def remote(src, dst, send, recv, device):
        return pltpu.make_async_remote_copy(
            src_ref=src, dst_ref=dst, send_sem=send, recv_sem=recv, device_id=device,
            device_id_type=pl.DeviceIdType.MESH,
        )

    signal(mate)
    signal(opposite)
    for step in range(1, chips):
        signal(along_x(step))
    for step in range(1, time_ways):
        signal((a, along_time(step)))

    data[0, 0:3] = pos_ref[...].astype(jnp.float32)
    data[0, 3:6] = vel_ref[...].astype(jnp.float32)
    for slot in range(wide.shape[0]):
        for lag in range(LAGS):
            wide[slot, time_ways * frames + lag] = jnp.zeros(wide.shape[2:], jnp.float32)
    pl.semaphore_wait(pltpu.get_barrier_semaphore(), chips + time_ways)

    def shipped(step):
        return remote(data.at[0], data.at[2 * step], x_send.at[step], in_recv.at[2 * step], along_x(step))

    def relayed(p):
        return remote(
            data.at[2 * p], data.at[2 * p + 1], relay_send.at[p], in_recv.at[2 * p + 1], mate
        )

    def mode_copy(step, f, count):
        goal, at = along_time(step), pl.ds(f, count)
        return remote(
            stage.at[goal, at], series.at[t, at], mode_send.at[step], mode_recv.at[step], (a, goal)
        )

    def mode_arrival(step):
        source = (t + time_ways - step) % time_ways
        return remote(
            stage.at[source], series.at[source], mode_send.at[step], mode_recv.at[step], (a, source)
        )

    for step in range(1, chips):
        shipped(step).start()

    blocks = data.shape[3] // LANES

    def tables(p):
        if p > 0:
            shipped(p).wait_recv()
        relayed(p).start()
        prepare(data, 2 * p, 2 * p * blocks, xs, yc, ys, zc, zs, first_w, group, y_waves)
        relayed(p).wait_recv()
        prepare(data, 2 * p + 1, (2 * p + 1) * blocks, xs, yc, ys, zc, zs, first_w, group, y_waves)

    def product(f, p):
        return frame_product(f, data, p, xs, yc, ys, zc, zs, min(16 * LANES, data.shape[3]), group, rows)

    def emit(f):
        for j, block in enumerate(combine(total[f], group, rows)):
            block = block.astype(stage.dtype)
            for k in range(split):
                stage[j * split + k, f] = block[k * owned : (k + 1) * owned]
        series[t, f] = stage[t, f]
        for step in range(1, time_ways):
            mode_copy(step, f, 1).start()

    early = frames * 5 // 8

    def own_part(f, _):
        total[f] = product(f, 0)
        return 0

    tables(0)
    lax.fori_loop(0, early, own_part, 0)
    for p in range(1, chips):
        tables(p)

        def far_part(f, _):
            total[f] += product(f, p)
            if p == chips - 1:
                emit(f)
            return 0

        lax.fori_loop(0, early, far_part, 0)

    def whole_frame(f, _):
        total[f] = jnp.zeros(total.shape[1:], jnp.float32)

        def part(p, _):
            total[f] += product(f, p)
            return 0

        lax.fori_loop(0, chips, part, 0)
        emit(f)
        return 0

    lax.fori_loop(early, frames, whole_frame, 0)

    widen(series, t, wide)
    for step in range(1, time_ways):
        mode_arrival(step).wait_recv()
        widen(series, (t + time_ways - step) % time_ways, wide)

    own_fold, mirror_fold = fold_matrices()
    tall = wide.shape[2]
    half = owned * KZ
    span = tall * KZ
    swaps = []
    for r in range(owned // tall):
        correlate(wide, sums, r, time_ways * frames, tall, atoms)
        at = half - (r + 1) * span
        arrange(sums, folded, mirror_fold, mirror, at, tall, True)
        swap = remote(
            mirror.at[:, :, pl.ds(at, span)], out_ref.at[:, :, pl.ds(at, span)],
            mirror_send.at[r], mirror_recv.at[r], opposite,
        )
        swap.start()
        swaps.append(swap)
        arrange(sums, folded, own_fold, out_ref, half + r * span, tall, False)

    for step in range(1, time_ways):
        mode_copy(step, 0, frames).wait_send()
    for step in range(1, chips):
        shipped(step).wait_send()
    for p in range(chips):
        relayed(p).wait_send()
    for swap in swaps:
        swap.wait()


def call(positions, velocity, atom_ways, time_ways, rows, y_waves):
    frames, lanes = positions.shape[1], positions.shape[2]
    atoms = lanes * atom_ways
    group = KX // atom_ways
    blocks = atom_ways * lanes // LANES
    tall = min(8, rows)
    dims = (atom_ways, time_ways, y_waves, atoms)
    whole = pl.BlockSpec(memory_space=pltpu.VMEM)
    dma = pltpu.SemaphoreType.DMA
    tabled = pltpu.VMEM((blocks, KY // 2 * (frames + 1), LANES), jnp.float32)
    return pl.pallas_call(
        functools.partial(kernel, dims),
        out_shape=jax.ShapeDtypeStruct((COMPS, LAGS, 2 * rows * KZ), jnp.float32),
        in_specs=[whole, whole],
        out_specs=whole,
        scratch_shapes=[
            pltpu.VMEM((atom_ways, 6, frames, lanes), jnp.float32),
            pltpu.VMEM((blocks, 2 * (group - (group - 1) // 2) + COMPS - 1, frames, LANES), jnp.float32),
            tabled, tabled, tabled, tabled,
            pltpu.VMEM((frames, group * KY, LANES), jnp.float32),
            pltpu.VMEM((time_ways, frames, rows, 2 * LANES), WIRE),
            pltpu.VMEM((time_ways, frames, rows, 2 * LANES), WIRE),
            pltpu.VMEM((2 * (rows // tall), time_ways * frames + LAGS, tall, LANES), jnp.float32),
            pltpu.VMEM((2, LAGS * tall, LANES), jnp.float32),
            pltpu.VMEM((LAGS * tall, LANES), jnp.float32),
            pltpu.VMEM((COMPS, LAGS, rows * KZ), jnp.float32),
            dma((atom_ways,)),
            dma((atom_ways // 2,)),
            dma((atom_ways // 2,)),
            dma((time_ways,)),
            dma((time_ways,)),
            dma((rows // tall,)),
            dma((rows // tall,)),
        ],
        compiler_params=pltpu.CompilerParams(
            vmem_limit_bytes=VMEM, collective_id=0, has_side_effects=True
        ),
        name="factors",
    )(positions, velocity)


def per_device(positions, velocity):
    atom_ways = lax.axis_size("atom")
    time_ways = lax.axis_size("tm")
    owned = KX * KY // (atom_ways * time_ways)
    rows = owned // 2
    y_waves = [wave(q, KY) for q in range(KY) if q % owned >= rows]
    positions, velocity = (jnp.transpose(v, (1, 0, 2)) for v in (positions, velocity))
    return call(positions, velocity, atom_ways, time_ways, rows, y_waves)


def solution(mesh):
    in_specs = (P("tm", None, "atom"), P("tm", None, "atom"))
    out_specs = P(None, None, ("atom", "tm"))
    return jax.shard_map(
        per_device, mesh=mesh, in_specs=in_specs, out_specs=out_specs, check_vma=False
    )
```
